128 devices in a mesh: pipe: 4 (over y), expert: 32 (over z, x, core).
Axes of the slice: x: 4, y: 4, z: 4, core: 2. Of those that a mesh axis runs over, the one named last changes fastest.
Arguments:
- forward_input: bfloat16 [4, 4096, 3584], P('pipe', 'expert'), may hold values from -45 to 45
- forward_routes: int32 [4, 4096, 2], P('pipe', 'expert'), may hold values from 0 to 31, as said below
- forward_gates: float32 [4, 4096, 2], P('pipe', 'expert'), may hold values from 0.3 to 3
- backward_input: bfloat16 [4, 4096, 3584], P('pipe', 'expert'), may hold values from -45 to 45
- backward_routes: int32 [4, 4096, 2], P('pipe', 'expert'), may hold values from 0 to 31, as said below
- backward_gates: float32 [4, 4096, 2], P('pipe', 'expert'), may hold values from 0.3 to 3
- upstream_gradient: bfloat16 [4, 4096, 3584], P('pipe', 'expert'), may hold values from -6 to 6
- norm_gain: bfloat16 [4, 3584], P('pipe'), may hold values from 0.5 to 2
- gate_weight: bfloat16 [4, 32, 3584, 1024], P('pipe', 'expert'), may hold values from -0.09375 to 0.09375
- up_weight: bfloat16 [4, 32, 3584, 1024], P('pipe', 'expert'), may hold values from -0.09375 to 0.09375
- down_weight: bfloat16 [4, 32, 1024, 3584], P('pipe', 'expert'), may hold values from -0.1875 to 0.1875
Outputs:
- forward_next: bfloat16 [4, 4096, 3584], P('pipe', 'expert')
- backward_next: bfloat16 [4, 4096, 3584], P('pipe', 'expert')
The draws below stay inside these ranges and needn't reach their ends.
Inputs may be any that keep to these rules, and one draw needn't show every extreme that they name: `forward_routes`: each token names 2 different experts. At every section, of the 128 tokens of one device at most 14 name any one expert, and one expert of the section is named by exactly 14 tokens of every device. `backward_routes`: each token names 2 different experts. At every section, of the 128 tokens of one device at most 14 name any one expert, and one expert of the section is named by exactly 14 tokens of every device.
All inputs are finite; a program needn't handle non-finite values.
Results may differ from the reference program's by a relative error of at most 0.0069.
Values may be sent and summed in bfloat16 or wider, within the bound.
A program may use at most 128 MiB of HBM per device.

```python
import math
import jax
import jax.numpy as jnp
from jax import lax

D = 3584
FE = 1024
TOP = 2
TOK_DEV = 128
EXPERTS = 32
MOST = 14
TOKENS = 4096
N_PIPE = 4
N_EXPERT = 32


def route_draw(key):
    first, second, third, fourth, fifth, sixth = jax.random.split(key, 6)
    routes_dev = TOK_DEV * TOP
    lowest = (routes_dev + N_EXPERT - 1) // N_EXPERT
    hottest = jax.random.randint(first, (N_PIPE, 1, 1), 0, N_EXPERT).astype(jnp.int32)
    experts = jnp.arange(N_EXPERT, dtype=jnp.int32)[None, None, :]
    scores = jax.random.randint(second, (N_PIPE, N_EXPERT, N_EXPERT), 0, 1 << 20).astype(jnp.int32) * N_EXPERT + experts
    scores = jnp.where(experts == hottest, -1, scores)
    order = jnp.argsort(scores, axis=2).astype(jnp.int32)
    caps = jax.random.randint(third, (N_PIPE, N_EXPERT, N_EXPERT), lowest, MOST + 1).astype(jnp.int32)
    forced = jax.random.randint(fourth, (N_PIPE, N_EXPERT, 1), 0, 2).astype(jnp.int32)
    caps = jnp.where((experts == 0) | (experts <= 2) & (forced == 1), MOST, caps)
    before = jnp.cumsum(caps, axis=2) - caps
    counts = jnp.clip(routes_dev - before, 0, caps)
    ends = jnp.cumsum(counts, axis=2)
    places = jnp.arange(routes_dev, dtype=jnp.int32)
    block_of = jnp.sum((ends[:, :, None, :] <= places[None, None, :, None]).astype(jnp.int32), axis=3)
    sequence = jnp.take_along_axis(order, block_of, axis=2)
    chosen = jnp.transpose(sequence.reshape(N_PIPE, N_EXPERT, TOP, TOK_DEV), (0, 1, 3, 2))
    column = jnp.arange(TOP, dtype=jnp.int32)[None, :]
    shuffle = jax.random.randint(fifth, (N_PIPE, N_EXPERT, TOK_DEV), 0, 1 << 20).astype(jnp.int32) * TOK_DEV + jnp.arange(TOK_DEV, dtype=jnp.int32)
    rows_order = jnp.argsort(shuffle, axis=2)
    chosen = jnp.take_along_axis(chosen, rows_order[..., None], axis=2)
    turns = jax.random.randint(sixth, (N_PIPE, N_EXPERT, TOK_DEV, 1), 0, TOP).astype(jnp.int32)
    chosen = jnp.take_along_axis(chosen, (column[None, None] + turns) % TOP, axis=3)
    return chosen.reshape(N_PIPE, N_EXPERT * TOK_DEV, TOP).astype(jnp.int32)


def activation_draw(key, low, high, base):
    first, second = jax.random.split(key, 2)
    row_scale = jnp.exp(jax.random.uniform(first, (N_PIPE, TOKENS, 1), minval=math.log(low), maxval=math.log(high)))
    col_scale = jnp.exp(jax.random.uniform(second, (N_PIPE, 1, D), minval=math.log(0.3), maxval=math.log(3.0)))
    return (base * row_scale * col_scale).astype(jnp.bfloat16)


def activation_base(key):
    low, high = (0.3, 3.0)
    base = jnp.clip(jax.random.normal(key, (N_PIPE, TOKENS, D)), -5.0, 5.0)
    return (low, high, base)


def draw_forward_routes(key, part):
    key = jax.random.fold_in(key, 11)
    return route_draw(key)


def draw_backward_routes(key, part):
    key = jax.random.fold_in(key, 12)
    return route_draw(key)


def draw_forward_input(key, part):
    key = jax.random.fold_in(key, 21)
    scales_key, base_key = jax.random.split(key, 2)
    low, high, base = activation_base(base_key)
    return activation_draw(scales_key, low, high, base)


def draw_backward_input(key, part):
    key = jax.random.fold_in(key, 22)
    scales_key, base_key = jax.random.split(key, 2)
    low, high, base = activation_base(base_key)
    return activation_draw(scales_key, low, high, base)


def level_of(stream_key, dims, shards, smallest, high):
    level, own = 1.0, jax.random.fold_in(stream_key, 6)
    for axis_at, blocks in shards:
        heights = jnp.exp(jax.random.uniform(jax.random.fold_in(own, axis_at), (blocks,), jnp.float32, smallest / len(shards), high / len(shards)))
        level = level * jnp.repeat(heights, dims[axis_at] // blocks).reshape([-1 if axis == axis_at else 1 for axis in range(len(dims))])
    return level


def scatter_about(own_key, extent, spread, bound, cuts=(), held_as=jnp.bfloat16):
    entries = jax.random.normal(own_key, extent, jnp.float32) * spread
    if len(cuts) > 0:
        entries = level_of(own_key, extent, cuts, -0.22, 0.18) * entries
    return jnp.clip(entries, min=-bound, max=bound).astype(held_as)


def setup_inputs(seed: int = 0) -> dict:
    seeds = jax.random.split(jax.random.key(seed), 12)
    forward_input = draw_forward_input(jax.random.fold_in(seeds[11], 71), 0)
    forward_routes = draw_forward_routes(jax.random.fold_in(seeds[11], 71), 0)
    forward_gates = jnp.clip(jnp.exp(math.log(3.0) - 2.3025851 * jax.random.uniform(seeds[2], (N_PIPE, TOKENS, TOP), jnp.float32) ** level_of(seeds[2], (N_PIPE, TOKENS, TOP), ((0, 4), (1, 32)), -0.2, 0.2)), 0.3, 3.0)
    backward_input = draw_backward_input(jax.random.fold_in(seeds[11], 71), 0)
    backward_routes = draw_backward_routes(jax.random.fold_in(seeds[11], 71), 0)
    backward_gates = jnp.clip(jnp.exp(math.log(3.0) - 2.3025851 * jax.random.uniform(seeds[5], (N_PIPE, TOKENS, TOP), jnp.float32) ** level_of(seeds[5], (N_PIPE, TOKENS, TOP), ((0, 4), (1, 32)), -0.2, 0.2)), 0.3, 3.0)
    upstream_gradient = scatter_about(seeds[6], (N_PIPE, TOKENS, D), 1.0, 6.0, ((0, 4), (1, 32)))
    norm_gain = jnp.clip(jnp.exp(math.log(2.0) - 1.3862944 * jax.random.uniform(seeds[7], (N_PIPE, D), jnp.float32) ** level_of(seeds[7], (N_PIPE, D), ((0, 4),), -0.2, 0.2)), 0.5, 2.0).astype(jnp.bfloat16)
    gate_weight = scatter_about(seeds[8], (N_PIPE, EXPERTS, D, FE), D ** -0.5, 0.09375, ((0, 4), (1, 32)))
    up_weight = scatter_about(seeds[9], (N_PIPE, EXPERTS, D, FE), D ** -0.5, 0.09375, ((0, 4), (1, 32)))
    down_weight = scatter_about(seeds[10], (N_PIPE, EXPERTS, FE, D), FE ** -0.5, 0.1875, ((0, 4), (1, 32)))
    return dict(forward_input=forward_input, forward_routes=forward_routes, forward_gates=forward_gates, backward_input=backward_input, backward_routes=backward_routes, backward_gates=backward_gates, upstream_gradient=upstream_gradient, norm_gain=norm_gain, gate_weight=gate_weight, up_weight=up_weight, down_weight=down_weight)


EPSILON = 1e-06

def normalize(block, gain_row):
    values = block.astype(jnp.float32)
    inverse_rms = lax.rsqrt(lax.optimization_barrier(jnp.mean(values * values, axis=-1, keepdims=True)) + EPSILON)
    normed = (values * inverse_rms * gain_row.astype(jnp.float32)).astype(jnp.bfloat16)
    return (values, inverse_rms, normed)

def product(left_arg, right_arg):
    return jnp.dot(left_arg.astype(jnp.float32), right_arg.astype(jnp.float32), preferred_element_type=jnp.float32)

def layout(choices_of):
    per_device = TOK_DEV * TOP
    expert_of = choices_of.reshape(N_EXPERT, per_device)
    onehot = (expert_of[:, :, None] == jnp.arange(N_EXPERT, dtype=jnp.int32)[None, None, :]).astype(jnp.int32)
    position = lax.optimization_barrier(jnp.sum((jnp.cumsum(onehot, axis=1) - onehot) * onehot, axis=2))
    sender = jnp.broadcast_to(jnp.arange(N_EXPERT, dtype=jnp.int32)[:, None], expert_of.shape)
    route_index = jnp.broadcast_to(jnp.arange(per_device, dtype=jnp.int32)[None, :], expert_of.shape)
    column = sender * MOST + position
    table = jnp.full((N_EXPERT, N_EXPERT * MOST), N_EXPERT * per_device, jnp.int32)
    table = table.at[expert_of, column].set(sender * per_device + route_index)
    return (expert_of, column, table)

def expert_forward(operands):
    block, gate_matrix, up_matrix, down_matrix = operands
    gate_pre = product(block, gate_matrix)
    up_pre = product(block, up_matrix)
    active = (gate_pre * jax.nn.sigmoid(gate_pre) * up_pre).astype(jnp.bfloat16)
    return product(active, down_matrix).astype(jnp.bfloat16)

def expert_backward(operands):
    block, grads, gate_matrix, up_matrix, down_matrix = operands
    gate_pre = product(block, gate_matrix)
    up_pre = product(block, up_matrix)
    sigmoid_gate = jax.nn.sigmoid(gate_pre)
    hidden = product(grads, down_matrix.T)
    gate_grad = (hidden * up_pre * sigmoid_gate * (1.0 + gate_pre * (1.0 - sigmoid_gate))).astype(jnp.bfloat16)
    up_grad = (hidden * gate_pre * sigmoid_gate).astype(jnp.bfloat16)
    return (product(gate_grad, gate_matrix.T) + product(up_grad, up_matrix.T)).astype(jnp.bfloat16)

def with_zero_row(block):
    return jnp.concatenate([block, jnp.zeros((1, block.shape[1]), block.dtype)], axis=0)

def reference(forward_input, forward_routes, forward_gates, backward_input, backward_routes, backward_gates, upstream_gradient, norm_gain, gate_weight, up_weight, down_weight):
    forward_layers = []
    backward_layers = []
    for section_index in range(N_PIPE):
        gain_row = norm_gain[section_index]
        values, inverse_rms, normed = normalize(forward_input[section_index], gain_row)
        expert_of, column, table = layout(forward_routes[section_index])
        gathered = with_zero_row(normed)[table // TOP]
        results = lax.map(expert_forward, (gathered, gate_weight[section_index], up_weight[section_index], down_weight[section_index]))
        picked = results[expert_of, column].reshape(TOKENS, TOP, D).astype(jnp.float32)
        mixed = values + lax.optimization_barrier(jnp.sum(forward_gates[section_index][:, :, None] * picked, axis=1))
        forward_layers.append(mixed.astype(jnp.bfloat16))
        stored, stored_rms, stored_normed = normalize(backward_input[section_index], gain_row)
        expert_back, column_back, table_back = layout(backward_routes[section_index])
        grad_out = upstream_gradient[section_index].astype(jnp.float32)
        route_grad = (backward_gates[section_index][:, :, None] * grad_out[:, None, :]).astype(jnp.bfloat16).reshape(TOKENS * TOP, D)
        gathered_rows = with_zero_row(stored_normed)[table_back // TOP]
        gathered_grads = with_zero_row(route_grad)[table_back]
        returned = lax.map(expert_backward, (gathered_rows, gathered_grads, gate_weight[section_index], up_weight[section_index], down_weight[section_index]))
        picked_back = returned[expert_back, column_back].reshape(TOKENS, TOP, D).astype(jnp.float32)
        normed_grad = gain_row.astype(jnp.float32) * lax.optimization_barrier(jnp.sum(picked_back, axis=1))
        cubed = stored_rms * stored_rms * stored_rms
        layer_grad = grad_out + stored_rms * normed_grad - stored * cubed * lax.optimization_barrier(jnp.mean(stored * normed_grad, axis=-1, keepdims=True))
        backward_layers.append(layer_grad.astype(jnp.bfloat16))
    forward_next = jnp.roll(jnp.stack(forward_layers), 1, axis=0)
    backward_next = jnp.roll(jnp.stack(backward_layers), -1, axis=0)
    return (forward_next, backward_next)
```

```python
import functools

import jax
import jax.numpy as jnp
from jax import lax
from jax.experimental import pallas as pl
from jax.experimental.pallas import tpu as pltpu
from jax.sharding import PartitionSpec as P

EPSILON = 1e-06
MESH = pl.DeviceIdType.MESH
BF = jnp.bfloat16
F32 = jnp.float32
D = 3584
FE = 1024
HALF = D // 2
QUARTER = D // 4
SIDE = 4
SLOTS = 14
CHUNKS = ((0, 512), (512, 384))
STEP = 256


def dot(a, b):
    return jnp.dot(a, b, preferred_element_type=F32)


def dot_nt(a, b):
    return lax.dot_general(a, b, (((1,), (1,)), ((), ())), preferred_element_type=F32)


def rows(value):
    return value.reshape(value.shape[-3] * value.shape[-2], value.shape[-1])


def tiles(value):
    return value.reshape(value.shape[0] // 16, 16, value.shape[1])


def split(value):
    high = value.astype(BF)
    return high, (value - high.astype(F32)).astype(BF)


def kernel(
    rg, fin, bin_, upg, gain, wg, wu, wd, fo, bo,
    WG, WU, WD, G, XA, YB, S, L, OWN, RG, PA, PB, GG, UG, PERM, TRI, EYE,
    s_rg_r, s_rg_s, s_g_r, s_g_s, s_x_r, s_x_s, s_r_r, s_r_s,
    s_t1_r, s_t1_s, s_t2_r, s_t2_s, s_c_r, s_y_r, s_y_s, s_w, s_o, s_l,
):
    pipe = lax.axis_index("pipe")
    me = lax.axis_index("expert")
    core = lax.rem(me, 2)
    other = 1 - core
    ring = (lax.rem(me // 2, SIDE), me // (2 * SIDE))
    X = (XA, YB)

    def at(h, delta):
        return lax.rem(ring[h] + delta, SIDE)

    def dev(h, delta, k):
        r = at(h, delta)
        if h == 0:
            return (pipe, (ring[1] * SIDE + r) * 2 + k)
        return (pipe, (r * SIDE + ring[0]) * 2 + k)

    def cols(h, q, c0=0, cw=QUARTER):
        return pl.ds(pl.multiple_of(h * HALF + q * QUARTER + c0, 128), cw)

    def qcols(q, c0=0, cw=QUARTER):
        return pl.ds(pl.multiple_of(q * QUARTER + c0, 128), cw)

    def send(src, dst, ss, rs, device):
        pltpu.make_async_remote_copy(
            src_ref=src, dst_ref=dst, send_sem=ss, recv_sem=rs, device_id=device, device_id_type=MESH
        ).start()

    def copy(src, dst, sem):
        pltpu.make_async_copy(src, dst, sem).start()

    def wait(ref, sem):
        pltpu.make_async_copy(ref, ref, sem).wait()

    copy(upg, OWN.at[0], s_o.at[0])
    copy(bin_, OWN.at[1], s_o.at[1])
    copy(fin, OWN.at[2], s_o.at[2])

    barrier = pltpu.get_barrier_semaphore()
    peers = [dev(h, d, k) for h in (0, 1) for d in (1, 2, 3) for k in (0, 1)]
    peers.append(dev(0, 0, other))
    ahead = (lax.rem(pipe + 1, SIDE), me)
    behind = (lax.rem(pipe + 3, SIDE), me)
    peers += [ahead, behind]
    for peer in peers:
        pl.semaphore_signal(barrier, inc=1, device_id=peer, device_id_type=MESH)
    pl.semaphore_wait(barrier, len(peers))

    for h in (0, 1):
        mine = ring[h] * 2 + core
        for d in (1, 2, 3):
            for k in (0, 1):
                send(rg, RG.at[h, mine], s_rg_s.at[h], s_rg_r.at[h], dev(h, d, k))
        send(rg, RG.at[h, mine], s_rg_s.at[h], s_rg_r.at[h], dev(h, 0, other))
        copy(rg, RG.at[h, mine], s_rg_r.at[h])

    def gather_start(a):
        for h in (0, 1):
            mine = ring[h] * 2 + core
            for d, k in ((1, 0), (3, 1)):
                for q in (0, 1):
                    send(OWN.at[a, :, :, cols(h, q)], G.at[a, h, mine], s_g_s.at[a, h], s_g_r.at[a, h, k], dev(h, d, q))
            send(OWN.at[a, :, :, cols(h, other)], G.at[a, h, mine], s_g_s.at[a, h], s_g_r.at[a, h, 4], dev(h, 0, other))
            copy(OWN.at[a, :, :, cols(h, core)], G.at[a, h, mine], s_g_r.at[a, h, 5])

    def gather_forward(a):
        for h in (0, 1):
            left = 2 * at(h, 3)
            wait(G.at[a, h, pl.ds(left, 2)], s_g_r.at[a, h, 0])
            for k in (0, 1):
                part = G.at[a, h, left + k, pl.ds(0, 4)]
                send(part, part, s_g_s.at[a, h], s_g_r.at[a, h, 2], dev(h, 1, core))
        for h in (0, 1):
            right = 2 * at(h, 1)
            wait(G.at[a, h, pl.ds(right, 2)], s_g_r.at[a, h, 1])
            for k in (0, 1):
                part = G.at[a, h, right + k, pl.ds(4, 4)]
                send(part, part, s_g_s.at[a, h], s_g_r.at[a, h, 3], dev(h, 3, core))

    def gather_finish(a, h):
        far = 2 * at(h, 2)
        wait(G.at[a, h, pl.ds(far, 2), pl.ds(0, 4)], s_g_r.at[a, h, 2])
        wait(G.at[a, h, pl.ds(far, 2), pl.ds(4, 4)], s_g_r.at[a, h, 3])
        wait(G.at[a, h, ring[h] * 2 + other], s_g_r.at[a, h, 4])
        wait(G.at[a, h, ring[h] * 2 + core], s_g_r.at[a, h, 5])

    def gather_sent(a):
        for h in (0, 1):
            wait(G.at[a, h, pl.ds(0, 7)], s_g_s.at[a, h])

    def normalize(a):
        def body(k, carry):
            v = OWN[a, k].astype(F32)
            r = lax.rsqrt(jnp.mean(v * v, axis=-1, keepdims=True) + EPSILON)
            OWN[a, k] = (v * r * gain[...]).astype(BF)
            return carry

        lax.fori_loop(0, 8, body, 0)

    wait(OWN.at[0], s_o.at[0])
    gather_start(0)
    wait(OWN.at[1], s_o.at[1])
    normalize(1)
    gather_start(1)
    copy(wg, WG, s_w.at[0])
    copy(wu, WU, s_w.at[1])
    copy(wd, WD, s_w.at[2])
    wait(OWN.at[2], s_o.at[2])
    normalize(2)

    up = lax.broadcasted_iota(jnp.int32, (128, 128), 0)
    across = lax.broadcasted_iota(jnp.int32, (128, 128), 1)
    TRI[...] = jnp.where(up < across, 1.0, 0.0).astype(BF)
    EYE[...] = jnp.where(up == across, 1.0, 0.0).astype(BF)
    line = lax.broadcasted_iota(jnp.int32, (448, 448), 0)
    outer = (line >= 112).astype(jnp.int32) + (line >= 224).astype(jnp.int32) + (line >= 336).astype(jnp.int32)
    rest = line - 112 * outer
    inner = (rest >= 28).astype(jnp.int32) + (rest >= 56).astype(jnp.int32) + (rest >= 84).astype(jnp.int32)
    place = 112 * inner + 28 * outer + rest - 28 * inner
    PERM[...] = jnp.where(lax.broadcasted_iota(jnp.int32, (448, 448), 1) == place, 1.0, 0.0).astype(BF)

    def experts(h):
        e = up // 16
        if h == 0:
            ids = (e // 2) * (2 * SIDE) + ring[0] * 2 + e % 2
        else:
            ids = ring[1] * (2 * SIDE) + e
        return ids.astype(F32)

    ids = [experts(h) for h in (0, 1)]
    in_tile = (up % 16).astype(F32)

    def route_row(h, s, row):
        return RG[h, s, pl.ds(row, 1), :]

    def build(st, h):
        def body(s, carry):
            named = (route_row(h, s, 4 * st) == ids[h]) | (route_row(h, s, 4 * st + 1) == ids[h])
            mask = jnp.where(named, 1.0, 0.0)
            before = dot(mask.astype(BF), TRI[...])
            first = 2.0 * s.astype(F32) + in_tile
            PA[st, h, s] = jnp.where(before == first, mask, 0.0).astype(BF)
            PB[st, h, s] = jnp.where(before == first - 16.0, mask, 0.0).astype(BF)
            return carry

        lax.fori_loop(0, 8, body, 0)

    def gates(st, h, s):
        return jnp.where(route_row(h, s, 4 * st) == ids[h], route_row(h, s, 4 * st + 2), route_row(h, s, 4 * st + 3))

    for h in (0, 1):
        wait(RG.at[h], s_rg_r.at[h])
    for st in (1, 0):
        for h in (0, 1):
            build(st, h)

    def pack(a, st, h, b, gated):
        def body(i, carry):
            both = rows(G[a, h, pl.ds(i, 2)].reshape(16, 16, QUARTER))
            pick = jnp.concatenate([PA[st, h, i], PB[st, h, i + 1]], axis=1)
            if gated:
                weight = jnp.concatenate([gates(st, h, i), gates(st, h, i + 1)], axis=1)
                high, low = split(pick.astype(F32) * weight)
                out = dot(high, both) + dot(low, both)
            else:
                out = dot(pick, both)
            S[b, h, :, i] = tiles(out.astype(BF))
            return carry

        lax.fori_loop(0, 7, body, 0)

    def scatter_start(a, h, b):
        place_at = pl.ds(7 * ring[1 - h], 7)
        for d in (1, 3, 2):
            for k in (0, 1):
                send(
                    S.at[b, h, 2 * at(1 - h, d) + k, pl.ds(0, 7)], X[h].at[a, place_at, :, qcols(core)],
                    s_x_s.at[a, h], s_x_r.at[a, h], dev(1 - h, d, k),
                )
        send(
            S.at[b, h, 2 * ring[1 - h] + other, pl.ds(0, 7)], X[h].at[a, place_at, :, qcols(core)],
            s_x_s.at[a, h], s_x_r.at[a, h], dev(1 - h, 0, other),
        )
        copy(S.at[b, h, 2 * ring[1 - h] + core, pl.ds(0, 7)], X[h].at[a, place_at, :, qcols(core)], s_l.at[a, h])

    def scatter_sent(a, b):
        for h in (0, 1):
            wait(S.at[b, h, pl.ds(0, 7), pl.ds(0, 7)], s_x_s.at[a, h])
            wait(S.at[b, h, 0, pl.ds(0, 7)], s_l.at[a, h])

    def scatter_finish(a, b):
        for h in (0, 1):
            wait(S.at[b, h, pl.ds(0, 7), pl.ds(0, 7)], s_x_r.at[a, h])

    gather_forward(0)
    for h in (0, 1):
        gather_finish(0, h)
        pack(0, 1, h, 0, True)
        scatter_start(0, h, 0)
    gather_start(2)
    gather_forward(1)
    gather_sent(0)
    for h in (0, 1):
        gather_finish(1, h)
        pack(1, 1, h, 1, False)
        scatter_start(1, h, 1)
    gather_forward(2)
    gather_sent(1)
    scatter_sent(0, 0)
    for h in (0, 1):
        gather_finish(2, h)
        pack(2, 0, h, 0, False)
    gather_sent(2)
    for h in (0, 1):
        scatter_start(2, h, 0)

    def exchange(a):
        def body(n, carry):
            at_cols = pl.ds(pl.multiple_of(n * STEP, STEP), STEP)
            YB[a, :, :, at_cols] = tiles(dot(PERM[...], rows(YB[a, :, :, at_cols])).astype(BF))
            return carry

        lax.fori_loop(0, HALF // STEP, body, 0)

    def exchange_hidden(src, dst):
        def body(n, carry):
            at_cols = pl.ds(pl.multiple_of(n * STEP, STEP), STEP)
            dst[1, :, :, at_cols] = tiles(dot(PERM[...], src[:, at_cols]).astype(BF))
            return carry

        lax.fori_loop(0, FE // STEP, body, 0)

    scatter_finish(0, 0)
    exchange(0)
    wait(WG, s_w.at[0])
    wait(WU, s_w.at[1])
    wait(WD, s_w.at[2])
    scatter_finish(1, 1)
    scatter_sent(1, 1)
    exchange(1)

    def into(a, W, at_cols):
        return dot(rows(XA[a]), W[pl.ds(0, HALF), at_cols]) + dot(rows(YB[a]), W[pl.ds(HALF, HALF), at_cols])

    def backward_hidden(f, carry):
        at_cols = pl.ds(pl.multiple_of(f * STEP, STEP), STEP)
        pre_gate = into(1, WG, at_cols)
        pre_up = into(1, WU, at_cols)
        hidden = dot_nt(rows(XA[0]), WD[at_cols, pl.ds(0, HALF)]) + dot_nt(rows(YB[0]), WD[at_cols, pl.ds(HALF, HALF)])
        sig = 1.0 / (1.0 + jnp.exp(-pre_gate))
        GG[:, at_cols] = (hidden * pre_up * sig * (1.0 + pre_gate * (1.0 - sig))).astype(BF)
        UG[:, at_cols] = (hidden * pre_gate * sig).astype(BF)
        return carry

    lax.fori_loop(0, FE // STEP, backward_hidden, 0)
    exchange_hidden(GG, XA)
    exchange_hidden(UG, YB)

    def return_start(b, ch, h, a):
        c0, cw = ((0, QUARTER),) [0] if b == 0 else CHUNKS[ch]
        gb = b
        mine = 2 * ring[1 - h] + core
        n = b * len(CHUNKS) + ch
        dst = G.at[gb, h, pl.ds(0, 7), mine, :, pl.ds(c0, cw)]
        for d in (1, 3, 2):
            for q in (0, 1):
                send(
                    X[h].at[a, pl.ds(7 * at(1 - h, d), 7), :, qcols(q, c0, cw)], dst,
                    s_r_s.at[n, h], s_r_r.at[n, h], dev(1 - h, d, q),
                )
        home = pl.ds(7 * ring[1 - h], 7)
        send(X[h].at[a, home, :, qcols(other, c0, cw)], dst, s_r_s.at[n, h], s_r_r.at[n, h], dev(1 - h, 0, other))
        copy(X[h].at[a, home, :, qcols(core, c0, cw)], dst, s_r_r.at[n, h])

    for h in (0, 1):

        def backward_out(n, carry):
            at_rows = pl.ds(pl.multiple_of(h * HALF + n * STEP, STEP), STEP)
            at_cols = pl.ds(pl.multiple_of(n * STEP, STEP), STEP)
            if h == 0:
                gg, ug = GG[...], UG[...]
            else:
                gg, ug = rows(XA[1, :, :, pl.ds(0, FE)]), rows(YB[1, :, :, pl.ds(0, FE)])
            X[h][0, :, :, at_cols] = tiles((dot_nt(gg, WG[at_rows, :]) + dot_nt(ug, WU[at_rows, :])).astype(BF))
            return carry

        lax.fori_loop(0, HALF // STEP, backward_out, 0)
        return_start(0, 0, h, 0)

    scatter_finish(2, 0)
    scatter_sent(2, 0)
    exchange(2)

    def forward_hidden(f, carry):
        at_cols = pl.ds(pl.multiple_of(f * STEP, STEP), STEP)
        pre_gate = into(2, WG, at_cols)
        pre_up = into(2, WU, at_cols)
        GG[:, at_cols] = (pre_gate * pre_up / (1.0 + jnp.exp(-pre_gate))).astype(BF)
        return carry

    lax.fori_loop(0, FE // STEP, forward_hidden, 0)
    exchange_hidden(GG, XA)
    for ch, (c0, cw) in enumerate(CHUNKS):
        for h in (0, 1):
            for q in (0, 1):
                for n in range(0, cw, STEP):
                    w = min(STEP, cw - n)
                    act = GG[...] if h == 0 else rows(XA[1, :, :, pl.ds(0, FE)])
                    start = q * QUARTER + c0 + n
                    X[h][2, :, :, pl.ds(start, w)] = tiles(dot(act, WD[:, pl.ds(h * HALF + start, w)]).astype(BF))
            return_start(1, ch, h, 2)

    copy(bin_, OWN.at[1], s_o.at[1])
    copy(fin, OWN.at[2], s_o.at[2])

    def combine(b, ch, h):
        c0, cw = (0, QUARTER) if b == 0 else CHUNKS[ch]
        st, to = (1, 1) if b == 0 else (0, 0)
        here = pl.ds(c0, cw)

        def body(s, carry):
            prev = rows(G[b, h, jnp.maximum(s - 1, 0), :, :, here])
            cur = rows(G[b, h, jnp.minimum(s, 6), :, :, here])
            pa, pb = PA[st, h, s], PB[st, h, s]
            if b == 0:
                out = dot(dot_nt(EYE[...], pb).astype(BF), prev) + dot(dot_nt(EYE[...], pa).astype(BF), cur)
            else:
                weight = gates(st, h, s)
                out = 0.0
                for pick, block in ((pb, prev), (pa, cur)):
                    for part in split(pick.astype(F32) * weight):
                        out = out + dot(dot_nt(EYE[...], part).astype(BF), block)
            S[to, h, s, :, :, here] = tiles(out.astype(BF))
            return carry

        lax.fori_loop(0, 8, body, 0)

    def land(b):
        return L if b == 0 else G.at[2]

    def meta(b, ch):
        c0, cw = (0, QUARTER) if b == 0 else CHUNKS[ch]
        return b * len(CHUNKS) + ch, pl.ds(c0, cw), (1 if b == 0 else 0), land(b)

    def far_start(b, ch, h):
        n, here, to, B = meta(b, ch)
        far = 2 * at(h, 2)
        for k in (0, 1):
            send(S.at[to, h, far + k, pl.ds(0, 4), :, here], B.at[h, 6, pl.ds(4 * k, 4), :, here], s_t1_s.at[n, h], s_t1_r.at[n, h, 0], dev(h, 1, core))
            send(S.at[to, h, far + k, pl.ds(4, 4), :, here], B.at[h, 7, pl.ds(4 * k, 4), :, here], s_t1_s.at[n, h], s_t1_r.at[n, h, 1], dev(h, 3, core))
        send(S.at[to, h, 2 * ring[h] + other, :, :, here], B.at[h, 4 + core, :, :, here], s_t2_s.at[n, h], s_c_r.at[n, h, 0], dev(h, 0, other))
        copy(S.at[to, h, 2 * ring[h] + core, :, :, here], B.at[h, 4 + core, :, :, here], s_c_r.at[n, h, 1])

    def near_start(b, ch, h):
        n, here, to, B = meta(b, ch)
        for slot, d, t0, base in ((6, 1, 0, 0), (7, 3, 4, 2)):
            wait(B.at[h, slot, :, :, here], s_t1_r.at[n, h, slot - 6])
            near = 2 * at(h, d)
            for k in (0, 1):
                own = S[to, h, near + k, pl.ds(t0, 4), :, here].astype(F32)
                got = B[h, slot, pl.ds(4 * k, 4), :, here].astype(F32)
                S[to, h, near + k, pl.ds(t0, 4), :, here] = (own + got).astype(BF)
                send(S.at[to, h, near + k, :, :, here], B.at[h, base + core, :, :, here], s_t2_s.at[n, h], s_t2_r.at[n, h], dev(h, d, k))

    def near_finish(b, ch, h):
        n, here, to, B = meta(b, ch)
        wait(B.at[h, pl.ds(0, 4), :, :, here], s_t2_r.at[n, h])
        wait(B.at[h, 4 + other, :, :, here], s_c_r.at[n, h, 0])
        wait(B.at[h, 4 + core, :, :, here], s_c_r.at[n, h, 1])

    def arrived(b, h, q, k, here):
        B = land(b)
        return B[h, q, k, :, here].astype(F32) + B[h, 2 + q, k, :, here].astype(F32) + B[h, 4 + q, k, :, here].astype(F32)

    for h in (0, 1):
        wait(G.at[0, h, pl.ds(0, 7)], s_r_r.at[0, h])
        combine(0, 0, h)
        far_start(0, 0, h)
    for h in (0, 1):
        near_start(0, 0, h)

    def forward_relay(ch):
        n, here, to, B = meta(1, ch)
        for h in (0, 1):
            wait(G.at[1, h, pl.ds(0, 7), :, :, here], s_r_r.at[n, h])
            combine(1, ch, h)
            far_start(1, ch, h)
        for h in (0, 1):
            near_start(1, ch, h)

    forward_relay(0)

    for h in (0, 1):
        near_finish(0, 0, h)
    wait(OWN.at[1], s_o.at[1])
    wait(OWN.at[2], s_o.at[2])

    def backward_last(k, carry):
        summed = jnp.concatenate([arrived(0, h, q, k, pl.ds(0, QUARTER)) for h in (0, 1) for q in (0, 1)], axis=1)
        stored = OWN[1, k].astype(F32)
        r = lax.rsqrt(jnp.mean(stored * stored, axis=-1, keepdims=True) + EPSILON)
        grad = gain[...] * summed
        mean = jnp.mean(stored * grad, axis=-1, keepdims=True)
        OWN[1, k] = (OWN[0, k].astype(F32) + r * grad - stored * (r * r * r) * mean).astype(BF)
        return carry

    lax.fori_loop(0, 8, backward_last, 0)
    send(OWN.at[1], bo, s_y_s.at[0], s_y_r.at[0], behind)

    def forward_last(ch):
        c0, cw = CHUNKS[ch]
        n, here, to, B = meta(1, ch)
        for h in (0, 1):
            near_finish(1, ch, h)

            def body(k, carry):
                for q in (0, 1):
                    spot = pl.ds(h * HALF + q * QUARTER + c0, cw)
                    OWN[2, k, :, spot] = (OWN[2, k, :, spot].astype(F32) + arrived(1, h, q, k, here)).astype(BF)
                return carry

            lax.fori_loop(0, 8, body, 0)
            for q in (0, 1):
                spot = pl.ds(h * HALF + q * QUARTER + c0, cw)
                send(OWN.at[2, :, :, spot], fo.at[:, :, spot], s_y_s.at[1 + ch], s_y_r.at[1 + ch], ahead)

    for ch in range(1, len(CHUNKS)):
        forward_relay(ch)
        forward_last(ch - 1)
    forward_last(len(CHUNKS) - 1)

    for h in (0, 1):
        wait(RG.at[h, pl.ds(0, 7)], s_rg_s.at[h])
    for b, chunks in ((0, ((0, QUARTER),)), (1, CHUNKS)):
        for ch, (c0, cw) in enumerate(chunks):
            n, here, to, B = meta(b, ch)
            for h in (0, 1):
                wait(S.at[to, h, pl.ds(0, 7), pl.ds(0, 7), :, here], s_r_s.at[n, h])
                wait(S.at[to, h, pl.ds(0, 2), :, :, here], s_t1_s.at[n, h])
                wait(S.at[to, h, pl.ds(0, 5), :, :, here], s_t2_s.at[n, h])
    wait(bo, s_y_s.at[0])
    wait(bo, s_y_r.at[0])
    for ch, (c0, cw) in enumerate(CHUNKS):
        wait(fo.at[:, :, pl.ds(0, 4 * cw)], s_y_s.at[1 + ch])
        wait(fo.at[:, :, pl.ds(0, 4 * cw)], s_y_r.at[1 + ch])


def local(
    forward_input,
    forward_routes,
    forward_gates,
    backward_input,
    backward_routes,
    backward_gates,
    upstream_gradient,
    norm_gain,
    gate_weight,
    up_weight,
    down_weight,
):
    rg = jnp.concatenate(
        [forward_routes[0].astype(F32), forward_gates[0], backward_routes[0].astype(F32), backward_gates[0]], axis=1
    ).T
    shape = (8, 16, D)
    parts = 1 + len(CHUNKS)
    groups = 2 * len(CHUNKS)
    dma = pltpu.SemaphoreType.DMA
    vmem = pl.BlockSpec(memory_space=pltpu.VMEM)
    anywhere = pl.BlockSpec(memory_space=pl.ANY)
    fo, bo = pl.pallas_call(
        kernel,
        name="relay",
        out_shape=(jax.ShapeDtypeStruct(shape, BF), jax.ShapeDtypeStruct(shape, BF)),
        in_specs=[vmem, anywhere, anywhere, anywhere, vmem, anywhere, anywhere, anywhere],
        out_specs=(anywhere, anywhere),
        scratch_shapes=[
            pltpu.VMEM((D, FE), BF),
            pltpu.VMEM((D, FE), BF),
            pltpu.VMEM((FE, D), BF),
            pltpu.VMEM((3, 2, 8, 8, 16, QUARTER), BF),
            pltpu.VMEM((3, 28, 16, HALF), BF),
            pltpu.VMEM((3, 28, 16, HALF), BF),
            pltpu.VMEM((2, 2, 8, 8, 16, QUARTER), BF),
            pltpu.VMEM((2, 8, 8, 16, QUARTER), BF),
            pltpu.VMEM((3, 8, 16, D), BF),
            pltpu.VMEM((2, 8, 8, 128), F32),
            pltpu.VMEM((2, 2, 8, 128, 128), BF),
            pltpu.VMEM((2, 2, 8, 128, 128), BF),
            pltpu.VMEM((448, FE), BF),
            pltpu.VMEM((448, FE), BF),
            pltpu.VMEM((448, 448), BF),
            pltpu.VMEM((128, 128), BF),
            pltpu.VMEM((128, 128), BF),
            dma((2,)),
            dma((2,)),
            dma((3, 2, 6)),
            dma((3, 2)),
            dma((3, 2)),
            dma((3, 2)),
            dma((groups, 2)),
            dma((groups, 2)),
            dma((groups, 2, 2)),
            dma((groups, 2)),
            dma((groups, 2)),
            dma((groups, 2)),
            dma((groups, 2, 2)),
            dma((parts,)),
            dma((parts,)),
            dma((3,)),
            dma((3,)),
            dma((3, 2)),
        ],
        compiler_params=pltpu.CompilerParams(
            collective_id=0, has_side_effects=True, vmem_limit_bytes=64 * 1024 * 1024 - 65536
        ),
        cost_estimate=pl.CostEstimate(flops=46 * 10**9, bytes_accessed=30 * 10**6, transcendentals=10**6),
    )(
        rg,
        forward_input.reshape(shape),
        backward_input.reshape(shape),
        upstream_gradient.reshape(shape),
        norm_gain.astype(F32),
        gate_weight[0, 0],
        up_weight[0, 0],
        down_weight[0, 0],
    )
    return (fo.reshape(1, 128, D), bo.reshape(1, 128, D))


def solution(mesh):
    rows_spec = P("pipe", "expert", None)
    weight = P("pipe", "expert", None, None)
    in_specs = (rows_spec,) * 7 + (P("pipe", None), weight, weight, weight)
    out_specs = (rows_spec, rows_spec)
    return jax.shard_map(local, mesh=mesh, in_specs=in_specs, out_specs=out_specs, check_vma=False)
```

```python
import functools

import jax
import jax.numpy as jnp
from jax import lax
from jax.experimental import pallas as pl
from jax.experimental.pallas import tpu as pltpu
from jax.sharding import PartitionSpec as P

EPSILON = 1e-06
MESH = pl.DeviceIdType.MESH
BF = jnp.bfloat16
F32 = jnp.float32
D = 3584
FE = 1024
HALF = D // 2
QUARTER = D // 4
SIDE = 4
SLOTS = 14
CHUNKS = ((0, 512), (512, 256), (768, 128))
STEP = 256


def dot(a, b):
    return jnp.dot(a, b, preferred_element_type=F32)


def dot_nt(a, b):
    return lax.dot_general(a, b, (((1,), (1,)), ((), ())), preferred_element_type=F32)


def rows(value):
    return value.reshape(value.shape[-3] * value.shape[-2], value.shape[-1])


def tiles(value):
    return value.reshape(value.shape[0] // 16, 16, value.shape[1])


def split(value):
    high = value.astype(BF)
    return high, (value - high.astype(F32)).astype(BF)


def kernel(
    fr, fg, br, bg, fin, bin_, upg, gain, wg, wu, wd, fo, bo,
    WG, WU, WD, G, XA, YB, S, L, OWN, RG, PA, PB, GG, UG, HID, PERM, TRI, EYE, PT, PG, rg,
    s_rg_r, s_rg_s, s_g_r, s_g_s, s_x_r, s_x_s, s_r_r, s_r_s,
    s_t1_r, s_t1_s, s_t2_r, s_t2_s, s_c_r, s_y_r, s_y_s, s_w, s_o, s_l,
):
    pipe = lax.axis_index("pipe")
    me = lax.axis_index("expert")
    core = lax.rem(me, 2)
    other = 1 - core
    ring = (lax.rem(me // 2, SIDE), me // (2 * SIDE))
    X = (XA, YB)

    def at(h, delta):
        return lax.rem(ring[h] + delta, SIDE)

    def dev(h, delta, k):
        r = at(h, delta)
        if h == 0:
            return (pipe, (ring[1] * SIDE + r) * 2 + k)
        return (pipe, (r * SIDE + ring[0]) * 2 + k)

    def cols(h, q, c0=0, cw=QUARTER):
        return pl.ds(pl.multiple_of(h * HALF + q * QUARTER + c0, 128), cw)

    def qcols(q, c0=0, cw=QUARTER):
        return pl.ds(pl.multiple_of(q * QUARTER + c0, 128), cw)

    def send(src, dst, ss, rs, device):
        pltpu.make_async_remote_copy(
            src_ref=src, dst_ref=dst, send_sem=ss, recv_sem=rs, device_id=device, device_id_type=MESH
        ).start()

    def copy(src, dst, sem):
        pltpu.make_async_copy(src, dst, sem).start()

    def wait(ref, sem):
        pltpu.make_async_copy(ref, ref, sem).wait()

    copy(upg, OWN.at[0], s_o.at[0])
    copy(bin_, OWN.at[1], s_o.at[1])
    copy(fin, OWN.at[2], s_o.at[2])

    rg[pl.ds(0, 2), :] = fr[...].astype(F32)
    rg[pl.ds(2, 2), :] = fg[...]
    rg[pl.ds(4, 2), :] = br[...].astype(F32)
    rg[pl.ds(6, 2), :] = bg[...]

    barrier = pltpu.get_barrier_semaphore()
    peers = [dev(h, d, k) for h in (0, 1) for d in (1, 2, 3) for k in (0, 1)]
    peers.append(dev(0, 0, other))
    ahead = (lax.rem(pipe + 1, SIDE), me)
    behind = (lax.rem(pipe + 3, SIDE), me)
    peers += [ahead, behind]
    for peer in peers:
        pl.semaphore_signal(barrier, inc=1, device_id=peer, device_id_type=MESH)
    def normalize(a):
        def body(k, carry):
            v = OWN[a, k].astype(F32)
            r = lax.rsqrt(jnp.mean(v * v, axis=-1, keepdims=True) + EPSILON)
            OWN[a, k] = (v * r * gain[...].astype(F32)).astype(BF)
            return carry

        lax.fori_loop(0, 8, body, 0)

    wait(OWN.at[1], s_o.at[1])
    normalize(1)
    up = lax.broadcasted_iota(jnp.int32, (128, 128), 0)
    across = lax.broadcasted_iota(jnp.int32, (128, 128), 1)
    TRI[...] = jnp.where(up < across, 1.0, 0.0).astype(BF)
    EYE[...] = jnp.where(up == across, 1.0, 0.0).astype(BF)
    line = lax.broadcasted_iota(jnp.int32, (448, 448), 0)
    outer = (line >= 112).astype(jnp.int32) + (line >= 224).astype(jnp.int32) + (line >= 336).astype(jnp.int32)
    rest = line - 112 * outer
    inner = (rest >= 28).astype(jnp.int32) + (rest >= 56).astype(jnp.int32) + (rest >= 84).astype(jnp.int32)
    place = 112 * inner + 28 * outer + rest - 28 * inner
    PERM[...] = jnp.where(lax.broadcasted_iota(jnp.int32, (448, 448), 1) == place, 1.0, 0.0).astype(BF)

    pl.semaphore_wait(barrier, len(peers))

    for h in (0, 1):
        mine = ring[h] * 2 + core
        for d in (1, 2, 3):
            for k in (0, 1):
                send(rg, RG.at[h, mine], s_rg_s.at[h], s_rg_r.at[h], dev(h, d, k))
        send(rg, RG.at[h, mine], s_rg_s.at[h], s_rg_r.at[h], dev(h, 0, other))
        copy(rg, RG.at[h, mine], s_rg_r.at[h])

    def gather_start(a):
        for h in (0, 1):
            mine = ring[h] * 2 + core
            for d, k in ((1, 0), (3, 1)):
                for q in (0, 1):
                    send(OWN.at[a, :, :, cols(h, q)], G.at[a, h, mine], s_g_s.at[a, h], s_g_r.at[a, h, k], dev(h, d, q))
            send(OWN.at[a, :, :, cols(h, other)], G.at[a, h, mine], s_g_s.at[a, h], s_g_r.at[a, h, 4], dev(h, 0, other))
            copy(OWN.at[a, :, :, cols(h, core)], G.at[a, h, mine], s_g_r.at[a, h, 5])

    def gather_forward(a):
        for h in (0, 1):
            left = 2 * at(h, 3)
            wait(G.at[a, h, pl.ds(left, 2)], s_g_r.at[a, h, 0])
            for k in (0, 1):
                part = G.at[a, h, left + k, pl.ds(0, 4)]
                send(part, part, s_g_s.at[a, h], s_g_r.at[a, h, 2], dev(h, 1, core))
        for h in (0, 1):
            right = 2 * at(h, 1)
            wait(G.at[a, h, pl.ds(right, 2)], s_g_r.at[a, h, 1])
            for k in (0, 1):
                part = G.at[a, h, right + k, pl.ds(4, 4)]
                send(part, part, s_g_s.at[a, h], s_g_r.at[a, h, 3], dev(h, 3, core))

    def gather_finish(a, h):
        far = 2 * at(h, 2)
        wait(G.at[a, h, pl.ds(far, 2), pl.ds(0, 4)], s_g_r.at[a, h, 2])
        wait(G.at[a, h, pl.ds(far, 2), pl.ds(4, 4)], s_g_r.at[a, h, 3])
        wait(G.at[a, h, ring[h] * 2 + other], s_g_r.at[a, h, 4])
        wait(G.at[a, h, ring[h] * 2 + core], s_g_r.at[a, h, 5])

    def gather_sent(a):
        for h in (0, 1):
            wait(G.at[a, h, pl.ds(0, 7)], s_g_s.at[a, h])

    wait(OWN.at[0], s_o.at[0])
    gather_start(0)
    copy(wd, WD, s_w.at[2])
    copy(wg, WG, s_w.at[0])
    copy(wu, WU, s_w.at[1])
    wait(OWN.at[2], s_o.at[2])
    normalize(2)

    def experts(h):
        e = up // 16
        if h == 0:
            ids = (e // 2) * (2 * SIDE) + ring[0] * 2 + e % 2
        else:
            ids = ring[1] * (2 * SIDE) + e
        return ids.astype(F32)

    ids = [experts(h) for h in (0, 1)]
    in_tile = (up % 16).astype(F32)

    def route_row(h, s, row):
        return RG[h, s, pl.ds(row, 1), :]

    def build(st, h):
        def body(s, carry):
            named = (route_row(h, s, 4 * st) == ids[h]) | (route_row(h, s, 4 * st + 1) == ids[h])
            mask = jnp.where(named, 1.0, 0.0)
            before = dot(mask.astype(BF), TRI[...])
            first = 2.0 * s.astype(F32) + in_tile
            PA[st, h, s] = jnp.where(before == first, mask, 0.0).astype(BF)
            PB[st, h, s] = jnp.where(before == first - 16.0, mask, 0.0).astype(BF)
            return carry

        lax.fori_loop(0, 8, body, 0)

    def gates(st, h, s):
        return jnp.where(route_row(h, s, 4 * st) == ids[h], route_row(h, s, 4 * st + 2), route_row(h, s, 4 * st + 3))

    for h in (0, 1):
        wait(RG.at[h], s_rg_r.at[h])
    for h in (0, 1):
        build(1, h)
    gather_start(1)
    for h in (0, 1):
        build(0, h)

    def pack(a, st, h, b, gated):
        def body(i, carry):
            both = rows(G[a, h, pl.ds(i, 2)].reshape(16, 16, QUARTER))
            pick = jnp.concatenate([PA[st, h, i], PB[st, h, i + 1]], axis=1)
            if gated:
                weight = jnp.concatenate([gates(st, h, i), gates(st, h, i + 1)], axis=1)
                high, low = split(pick.astype(F32) * weight)
                out = dot(high, both) + dot(low, both)
            else:
                out = dot(pick, both)
            S[b, h, :, i] = tiles(out.astype(BF))
            return carry

        lax.fori_loop(0, 7, body, 0)

    def scatter_start(a, h, b):
        place_at = pl.ds(7 * ring[1 - h], 7)
        for d in (1, 3, 2):
            for k in (0, 1):
                send(
                    S.at[b, h, 2 * at(1 - h, d) + k, pl.ds(0, 7)], X[h].at[a, place_at, :, qcols(core)],
                    s_x_s.at[a, h], s_x_r.at[a, h], dev(1 - h, d, k),
                )
        send(
            S.at[b, h, 2 * ring[1 - h] + other, pl.ds(0, 7)], X[h].at[a, place_at, :, qcols(core)],
            s_x_s.at[a, h], s_x_r.at[a, h], dev(1 - h, 0, other),
        )
        copy(S.at[b, h, 2 * ring[1 - h] + core, pl.ds(0, 7)], X[h].at[a, place_at, :, qcols(core)], s_l.at[a, h])

    def scatter_sent(a, b):
        for h in (0, 1):
            wait(S.at[b, h, pl.ds(0, 7), pl.ds(0, 7)], s_x_s.at[a, h])
            wait(S.at[b, h, 0, pl.ds(0, 7)], s_l.at[a, h])

    def scatter_finish(a, b):
        for h in (0, 1):
            wait(S.at[b, h, pl.ds(0, 7), pl.ds(0, 7)], s_x_r.at[a, h])

    gather_forward(0)
    for h in (0, 1):

        def turn(s, carry):
            for k, T in enumerate((PB, PA)):
                spot = pl.ds(128 * k, 128)
                PT[h, s, :, spot] = dot_nt(EYE[...], T[1, h, s]).astype(BF)
                for n, part in enumerate(split(T[0, h, s].astype(F32) * gates(0, h, s))):
                    PG[n, h, s, :, spot] = dot_nt(EYE[...], part).astype(BF)
            return carry

        lax.fori_loop(0, 8, turn, 0)

    gather_forward(1)
    gather_start(2)
    for h in (0, 1):
        gather_finish(0, h)
        pack(0, 1, h, 0, True)
        scatter_start(0, h, 0)
    gather_sent(0)
    for h in (0, 1):
        gather_finish(1, h)
        pack(1, 1, h, 1, False)
    gather_forward(2)
    for h in (0, 1):
        scatter_start(1, h, 1)
    gather_sent(1)
    scatter_sent(0, 0)
    for h in (0, 1):
        gather_finish(2, h)
        pack(2, 0, h, 0, False)
    gather_sent(2)
    for h in (0, 1):
        scatter_start(2, h, 0)

    def exchange(a):
        def body(n, carry):
            at_cols = pl.ds(pl.multiple_of(n * STEP, STEP), STEP)
            YB[a, :, :, at_cols] = tiles(dot(PERM[...], rows(YB[a, :, :, at_cols])).astype(BF))
            return carry

        lax.fori_loop(0, HALF // STEP, body, 0)

    def exchange_hidden(src, dst):
        def body(n, carry):
            at_cols = pl.ds(pl.multiple_of(n * STEP, STEP), STEP)
            dst[1, :, :, at_cols] = tiles(dot(PERM[...], src[:, at_cols]).astype(BF))
            return carry

        lax.fori_loop(0, FE // STEP, body, 0)

    scatter_finish(0, 0)
    exchange(0)
    wait(WD, s_w.at[2])

    def early_hidden(f, carry):
        at_cols = pl.ds(pl.multiple_of(f * STEP, STEP), STEP)
        HID[:, at_cols] = dot_nt(rows(XA[0]), WD[at_cols, pl.ds(0, HALF)]) + dot_nt(rows(YB[0]), WD[at_cols, pl.ds(HALF, HALF)])
        return carry

    lax.fori_loop(0, FE // STEP, early_hidden, 0)
    wait(WG, s_w.at[0])
    wait(WU, s_w.at[1])
    scatter_finish(1, 1)
    scatter_sent(1, 1)
    exchange(1)

    def into(a, W, at_cols):
        return dot(rows(XA[a]), W[pl.ds(0, HALF), at_cols]) + dot(rows(YB[a]), W[pl.ds(HALF, HALF), at_cols])

    def backward_hidden(f, carry):
        at_cols = pl.ds(pl.multiple_of(f * STEP, STEP), STEP)
        pre_gate = into(1, WG, at_cols)
        pre_up = into(1, WU, at_cols)
        hidden = HID[:, at_cols]
        sig = 1.0 / (1.0 + jnp.exp(-pre_gate))
        GG[:, at_cols] = (hidden * pre_up * sig * (1.0 + pre_gate * (1.0 - sig))).astype(BF)
        UG[:, at_cols] = (hidden * pre_gate * sig).astype(BF)
        return carry

    lax.fori_loop(0, FE // STEP, backward_hidden, 0)
    exchange_hidden(GG, XA)
    exchange_hidden(UG, YB)

    def return_start(b, ch, h, a):
        c0, cw = ((0, QUARTER),) [0] if b == 0 else CHUNKS[ch]
        gb = b
        mine = 2 * ring[1 - h] + core
        n = b * len(CHUNKS) + ch
        dst = G.at[gb, h, pl.ds(0, 7), mine, :, pl.ds(c0, cw)]
        for d in (1, 3, 2):
            for q in (0, 1):
                send(
                    X[h].at[a, pl.ds(7 * at(1 - h, d), 7), :, qcols(q, c0, cw)], dst,
                    s_r_s.at[n, h], s_r_r.at[n, h], dev(1 - h, d, q),
                )
        home = pl.ds(7 * ring[1 - h], 7)
        send(X[h].at[a, home, :, qcols(other, c0, cw)], dst, s_r_s.at[n, h], s_r_r.at[n, h], dev(1 - h, 0, other))
        copy(X[h].at[a, home, :, qcols(core, c0, cw)], dst, s_r_r.at[n, h])

    for h in (0, 1):

        def backward_out(n, carry):
            at_rows = pl.ds(pl.multiple_of(h * HALF + n * STEP, STEP), STEP)
            at_cols = pl.ds(pl.multiple_of(n * STEP, STEP), STEP)
            if h == 0:
                gg, ug = GG[...], UG[...]
            else:
                gg, ug = rows(XA[1, :, :, pl.ds(0, FE)]), rows(YB[1, :, :, pl.ds(0, FE)])
            X[h][0, :, :, at_cols] = tiles((dot_nt(gg, WG[at_rows, :]) + dot_nt(ug, WU[at_rows, :])).astype(BF))
            return carry

        lax.fori_loop(0, HALF // STEP, backward_out, 0)
        return_start(0, 0, h, 0)

    scatter_finish(2, 0)
    scatter_sent(2, 0)
    exchange(2)

    def forward_hidden(f, carry):
        at_cols = pl.ds(pl.multiple_of(f * STEP, STEP), STEP)
        pre_gate = into(2, WG, at_cols)
        pre_up = into(2, WU, at_cols)
        GG[:, at_cols] = (pre_gate * pre_up / (1.0 + jnp.exp(-pre_gate))).astype(BF)
        return carry

    lax.fori_loop(0, FE // STEP, forward_hidden, 0)
    exchange_hidden(GG, XA)
    def forward_out(ch):
        c0, cw = CHUNKS[ch]
        for h in (0, 1):
            for q in (0, 1):
                for n in range(0, cw, STEP):
                    w = min(STEP, cw - n)
                    act = GG[...] if h == 0 else rows(XA[1, :, :, pl.ds(0, FE)])
                    start = q * QUARTER + c0 + n
                    X[h][2, :, :, pl.ds(start, w)] = tiles(dot(act, WD[:, pl.ds(h * HALF + start, w)]).astype(BF))

    def forward_return(ch):
        for h in (0, 1):
            return_start(1, ch, h, 2)

    forward_out(0)
    forward_return(0)
    forward_out(1)
    forward_out(2)

    copy(bin_, OWN.at[1], s_o.at[1])
    copy(fin, OWN.at[2], s_o.at[2])

    def combine(b, ch, h, ds):
        c0, cw = (0, QUARTER) if b == 0 else CHUNKS[ch]
        to = 1 if b == 0 else 0
        here = pl.ds(c0, cw)
        for d in ds:
            for k in (0, 1):
                s = 2 * at(h, d) + k
                prev = rows(G[b, h, jnp.maximum(s - 1, 0), :, :, here])
                cur = rows(G[b, h, jnp.minimum(s, 6), :, :, here])
                both = jnp.concatenate([prev, cur], axis=0)
                if b == 0:
                    out = dot(PT[h, s], both)
                else:
                    out = dot(PG[0, h, s], both) + dot(PG[1, h, s], both)
                S[to, h, s, :, :, here] = tiles(out.astype(BF))

    def land(b):
        return L if b == 0 else G.at[2]

    def meta(b, ch):
        c0, cw = (0, QUARTER) if b == 0 else CHUNKS[ch]
        return b * len(CHUNKS) + ch, pl.ds(c0, cw), (1 if b == 0 else 0), land(b)

    def far_start(b, ch, h):
        n, here, to, B = meta(b, ch)
        far = 2 * at(h, 2)
        combine(b, ch, h, (2,))
        for k in (0, 1):
            send(S.at[to, h, far + k, pl.ds(0, 4), :, here], B.at[h, 6, pl.ds(4 * k, 4), :, here], s_t1_s.at[n, h], s_t1_r.at[n, h, 0], dev(h, 1, core))
            send(S.at[to, h, far + k, pl.ds(4, 4), :, here], B.at[h, 7, pl.ds(4 * k, 4), :, here], s_t1_s.at[n, h], s_t1_r.at[n, h, 1], dev(h, 3, core))

    def own_start(b, ch, h):
        n, here, to, B = meta(b, ch)
        combine(b, ch, h, (1, 3, 0))
        send(S.at[to, h, 2 * ring[h] + other, :, :, here], B.at[h, 4 + core, :, :, here], s_t2_s.at[n, h], s_c_r.at[n, h, 0], dev(h, 0, other))
        copy(S.at[to, h, 2 * ring[h] + core, :, :, here], B.at[h, 4 + core, :, :, here], s_c_r.at[n, h, 1])

    def near_start(b, ch, h):
        n, here, to, B = meta(b, ch)
        for slot, d, t0, base in ((6, 1, 0, 0), (7, 3, 4, 2)):
            wait(B.at[h, slot, :, :, here], s_t1_r.at[n, h, slot - 6])
            near = 2 * at(h, d)
            for k in (0, 1):
                own = S[to, h, near + k, pl.ds(t0, 4), :, here].astype(F32)
                got = B[h, slot, pl.ds(4 * k, 4), :, here].astype(F32)
                S[to, h, near + k, pl.ds(t0, 4), :, here] = (own + got).astype(BF)
                send(S.at[to, h, near + k, :, :, here], B.at[h, base + core, :, :, here], s_t2_s.at[n, h], s_t2_r.at[n, h], dev(h, d, k))

    def near_finish(b, ch, h):
        n, here, to, B = meta(b, ch)
        wait(B.at[h, pl.ds(0, 4), :, :, here], s_t2_r.at[n, h])
        wait(B.at[h, 4 + other, :, :, here], s_c_r.at[n, h, 0])
        wait(B.at[h, 4 + core, :, :, here], s_c_r.at[n, h, 1])

    def arrived(b, h, q, k, here):
        B = land(b)
        return B[h, q, k, :, here].astype(F32) + B[h, 2 + q, k, :, here].astype(F32) + B[h, 4 + q, k, :, here].astype(F32)

    for h in (0, 1):
        wait(G.at[0, h, pl.ds(0, 7)], s_r_r.at[0, h])
        far_start(0, 0, h)
    for h in (0, 1):
        own_start(0, 0, h)
    def relay_far(ch):
        n, here, to, B = meta(1, ch)
        for h in (0, 1):
            wait(G.at[1, h, pl.ds(0, 7), :, :, here], s_r_r.at[n, h])
            far_start(1, ch, h)
        for h in (0, 1):
            own_start(1, ch, h)

    def relay_near(ch):
        for h in (0, 1):
            near_start(1, ch, h)

    relay_far(0)
    for h in (0, 1):
        near_start(0, 0, h)
    relay_near(0)
    forward_return(1)
    forward_return(2)

    for h in (0, 1):
        near_finish(0, 0, h)
    wait(OWN.at[1], s_o.at[1])
    wait(OWN.at[2], s_o.at[2])

    def backward_last(k, carry):
        summed = jnp.concatenate([arrived(0, h, q, k, pl.ds(0, QUARTER)) for h in (0, 1) for q in (0, 1)], axis=1)
        stored = OWN[1, k].astype(F32)
        r = lax.rsqrt(jnp.mean(stored * stored, axis=-1, keepdims=True) + EPSILON)
        grad = gain[...].astype(F32) * summed
        mean = jnp.mean(stored * grad, axis=-1, keepdims=True)
        OWN[1, k] = (OWN[0, k].astype(F32) + r * grad - stored * (r * r * r) * mean).astype(BF)
        return carry

    lax.fori_loop(0, 8, backward_last, 0)
    send(OWN.at[1], bo, s_y_s.at[0], s_y_r.at[0], behind)

    def forward_last(ch):
        c0, cw = CHUNKS[ch]
        n, here, to, B = meta(1, ch)
        for h in (0, 1):
            near_finish(1, ch, h)

            def body(k, carry):
                for q in (0, 1):
                    spot = pl.ds(h * HALF + q * QUARTER + c0, cw)
                    OWN[2, k, :, spot] = (OWN[2, k, :, spot].astype(F32) + arrived(1, h, q, k, here)).astype(BF)
                return carry

            lax.fori_loop(0, 8, body, 0)
            for q in (0, 1):
                spot = pl.ds(h * HALF + q * QUARTER + c0, cw)
                send(OWN.at[2, :, :, spot], fo.at[:, :, spot], s_y_s.at[1 + ch], s_y_r.at[1 + ch], ahead)

    forward_last(0)
    relay_far(1)
    relay_far(2)
    relay_near(1)
    forward_last(1)
    relay_near(2)
    forward_last(2)

    for h in (0, 1):
        wait(RG.at[h, pl.ds(0, 7)], s_rg_s.at[h])
    for b, chunks in ((0, ((0, QUARTER),)), (1, CHUNKS)):
        for ch, (c0, cw) in enumerate(chunks):
            n, here, to, B = meta(b, ch)
            for h in (0, 1):
                wait(S.at[to, h, pl.ds(0, 7), pl.ds(0, 7), :, here], s_r_s.at[n, h])
                wait(S.at[to, h, pl.ds(0, 2), :, :, here], s_t1_s.at[n, h])
                wait(S.at[to, h, pl.ds(0, 5), :, :, here], s_t2_s.at[n, h])
    wait(bo, s_y_s.at[0])
    wait(bo, s_y_r.at[0])
    for ch, (c0, cw) in enumerate(CHUNKS):
        wait(fo.at[:, :, pl.ds(0, 4 * cw)], s_y_s.at[1 + ch])
        wait(fo.at[:, :, pl.ds(0, 4 * cw)], s_y_r.at[1 + ch])


def hand_over(fo, bo, f_out, b_out, held, sem):
    loads = [pltpu.make_async_copy(a, held.at[i], sem.at[i]) for i, a in enumerate((fo, bo))]
    stores = [pltpu.make_async_copy(held.at[i], a, sem.at[2 + i]) for i, a in enumerate((f_out, b_out))]
    for copy in loads:
        copy.start()
    for load, store in zip(loads, stores):
        load.wait()
        store.start()
    for copy in stores:
        copy.wait()


def local(
    forward_input,
    forward_routes,
    forward_gates,
    backward_input,
    backward_routes,
    backward_gates,
    upstream_gradient,
    norm_gain,
    gate_weight,
    up_weight,
    down_weight,
):
    shape = (8, 16, D)
    parts = 1 + len(CHUNKS)
    groups = 2 * len(CHUNKS)
    dma = pltpu.SemaphoreType.DMA
    vmem = pl.BlockSpec(memory_space=pltpu.VMEM)
    anywhere = pl.BlockSpec(memory_space=pl.ANY)
    fo, bo = pl.pallas_call(
        kernel,
        name="relay",
        out_shape=(jax.ShapeDtypeStruct(shape, BF), jax.ShapeDtypeStruct(shape, BF)),
        in_specs=[vmem] * 4 + [anywhere] * 3 + [vmem] + [anywhere] * 3,
        out_specs=(anywhere, anywhere),
        scratch_shapes=[
            pltpu.VMEM((D, FE), BF),
            pltpu.VMEM((D, FE), BF),
            pltpu.VMEM((FE, D), BF),
            pltpu.VMEM((3, 2, 8, 8, 16, QUARTER), BF),
            pltpu.VMEM((3, 28, 16, HALF), BF),
            pltpu.VMEM((3, 28, 16, HALF), BF),
            pltpu.VMEM((2, 2, 8, 8, 16, QUARTER), BF),
            pltpu.VMEM((2, 8, 8, 16, QUARTER), BF),
            pltpu.VMEM((3, 8, 16, D), BF),
            pltpu.VMEM((2, 8, 8, 128), F32),
            pltpu.VMEM((2, 2, 8, 128, 128), BF),
            pltpu.VMEM((2, 2, 8, 128, 128), BF),
            pltpu.VMEM((448, FE), BF),
            pltpu.VMEM((448, FE), BF),
            pltpu.VMEM((448, FE), F32),
            pltpu.VMEM((448, 448), BF),
            pltpu.VMEM((128, 128), BF),
            pltpu.VMEM((128, 128), BF),
            pltpu.VMEM((2, 8, 128, 256), BF),
            pltpu.VMEM((2, 2, 8, 128, 256), BF),
            pltpu.VMEM((8, 128), F32),
            dma((2,)),
            dma((2,)),
            dma((3, 2, 6)),
            dma((3, 2)),
            dma((3, 2)),
            dma((3, 2)),
            dma((groups, 2)),
            dma((groups, 2)),
            dma((groups, 2, 2)),
            dma((groups, 2)),
            dma((groups, 2)),
            dma((groups, 2)),
            dma((groups, 2, 2)),
            dma((parts,)),
            dma((parts,)),
            dma((3,)),
            dma((3,)),
            dma((3, 2)),
        ],
        compiler_params=pltpu.CompilerParams(
            collective_id=0, has_side_effects=True, vmem_limit_bytes=64 * 1024 * 1024 - 65536
        ),
        cost_estimate=pl.CostEstimate(flops=46 * 10**9, bytes_accessed=30 * 10**6, transcendentals=10**6),
    )(
        forward_routes[0].T,
        forward_gates[0].T,
        backward_routes[0].T,
        backward_gates[0].T,
        forward_input.reshape(shape),
        backward_input.reshape(shape),
        upstream_gradient.reshape(shape),
        norm_gain,
        gate_weight[0, 0],
        up_weight[0, 0],
        down_weight[0, 0],
    )
    fo, bo = pl.pallas_call(
        hand_over,
        name="results",
        out_shape=(jax.ShapeDtypeStruct(shape, BF), jax.ShapeDtypeStruct(shape, BF)),
        in_specs=[anywhere] * 2,
        out_specs=(anywhere, anywhere),
        scratch_shapes=[pltpu.VMEM((2,) + shape, BF), dma((4,))],
        cost_estimate=pl.CostEstimate(flops=0, bytes_accessed=4 * 10**6, transcendentals=0),
    )(fo, bo)
    return (fo.reshape(1, 128, D), bo.reshape(1, 128, D))


def solution(mesh):
    rows_spec = P("pipe", "expert", None)
    weight = P("pipe", "expert", None, None)
    in_specs = (rows_spec,) * 7 + (P("pipe", None), weight, weight, weight)
    out_specs = (rows_spec, rows_spec)
    return jax.shard_map(local, mesh=mesh, in_specs=in_specs, out_specs=out_specs, check_vma=False)
```

```python
import functools

import jax
import jax.numpy as jnp
from jax import lax
from jax.experimental import pallas as pl
from jax.experimental.pallas import tpu as pltpu
from jax.sharding import PartitionSpec as P

EPSILON = 1e-06
MESH = pl.DeviceIdType.MESH
BF = jnp.bfloat16
F32 = jnp.float32
D = 3584
FE = 1024
HALF = D // 2
QUARTER = D // 4
SIDE = 4
SLOTS = 14
CHUNKS = ((0, 384), (384, 256), (640, 128), (768, 128))
DIRECT = (2, 3)
STEP = 256
WIDE = 512


def dot(a, b):
    return jnp.dot(a, b, preferred_element_type=F32)


def dot_nt(a, b):
    return lax.dot_general(a, b, (((1,), (1,)), ((), ())), preferred_element_type=F32)


def rows(value):
    return value.reshape(value.shape[-3] * value.shape[-2], value.shape[-1])


def tiles(value):
    return value.reshape(value.shape[0] // 16, 16, value.shape[1])


def split(value):
    high = value.astype(BF)
    return high, (value - high.astype(F32)).astype(BF)


def kernel(
    fr, fg, br, bg, fin, bin_, upg, gain, wg, wu, wd, fo, bo,
    WG, WU, WD, G, XA, YB, S, L, OWN, RG, PA, PB, GG, UG, HID, PERM, TRI, EYE, PT, PG, rg,
    s_rg_r, s_rg_s, s_g_r, s_g_s, s_x_r, s_x_s, s_r_r, s_r_s,
    s_t1_r, s_t1_s, s_t2_r, s_t2_s, s_c_r, s_y_r, s_y_s, s_w, s_o, s_l,
):
    pipe = lax.axis_index("pipe")
    me = lax.axis_index("expert")
    core = lax.rem(me, 2)
    other = 1 - core
    ring = (lax.rem(me // 2, SIDE), me // (2 * SIDE))
    X = (XA, YB)

    def at(h, delta):
        return lax.rem(ring[h] + delta, SIDE)

    def dev(h, delta, k):
        r = at(h, delta)
        if h == 0:
            return (pipe, (ring[1] * SIDE + r) * 2 + k)
        return (pipe, (r * SIDE + ring[0]) * 2 + k)

    def cols(h, q, c0=0, cw=QUARTER):
        return pl.ds(pl.multiple_of(h * HALF + q * QUARTER + c0, 128), cw)

    def qcols(q, c0=0, cw=QUARTER):
        return pl.ds(pl.multiple_of(q * QUARTER + c0, 128), cw)

    def send(src, dst, ss, rs, device):
        pltpu.make_async_remote_copy(
            src_ref=src, dst_ref=dst, send_sem=ss, recv_sem=rs, device_id=device, device_id_type=MESH
        ).start()

    def copy(src, dst, sem):
        pltpu.make_async_copy(src, dst, sem).start()

    def wait(ref, sem):
        pltpu.make_async_copy(ref, ref, sem).wait()

    copy(upg, OWN.at[0], s_o.at[0])
    copy(bin_, OWN.at[1], s_o.at[1])
    copy(fin, OWN.at[2], s_o.at[2])

    rg[pl.ds(0, 2), :] = fr[...].astype(F32)
    rg[pl.ds(2, 2), :] = fg[...]
    rg[pl.ds(4, 2), :] = br[...].astype(F32)
    rg[pl.ds(6, 2), :] = bg[...]

    barrier = pltpu.get_barrier_semaphore()
    peers = [dev(h, d, k) for h in (0, 1) for d in (1, 2, 3) for k in (0, 1)]
    peers.append(dev(0, 0, other))
    ahead = (lax.rem(pipe + 1, SIDE), me)
    behind = (lax.rem(pipe + 3, SIDE), me)
    peers += [ahead, behind]
    for peer in peers:
        pl.semaphore_signal(barrier, inc=1, device_id=peer, device_id_type=MESH)
    def normalize(a):
        def body(k, carry):
            v = OWN[a, k].astype(F32)
            r = lax.rsqrt(jnp.mean(v * v, axis=-1, keepdims=True) + EPSILON)
            OWN[a, k] = (v * r * gain[...].astype(F32)).astype(BF)
            return carry

        lax.fori_loop(0, 8, body, 0)

    up = lax.broadcasted_iota(jnp.int32, (128, 128), 0)
    across = lax.broadcasted_iota(jnp.int32, (128, 128), 1)
    TRI[...] = jnp.where(up < across, 1.0, 0.0).astype(BF)
    EYE[...] = jnp.where(up == across, 1.0, 0.0).astype(BF)
    line = lax.broadcasted_iota(jnp.int32, (448, 448), 0)
    outer = (line >= 112).astype(jnp.int32) + (line >= 224).astype(jnp.int32) + (line >= 336).astype(jnp.int32)
    rest = line - 112 * outer
    inner = (rest >= 28).astype(jnp.int32) + (rest >= 56).astype(jnp.int32) + (rest >= 84).astype(jnp.int32)
    place = 112 * inner + 28 * outer + rest - 28 * inner
    PERM[...] = jnp.where(lax.broadcasted_iota(jnp.int32, (448, 448), 1) == place, 1.0, 0.0).astype(BF)

    pl.semaphore_wait(barrier, len(peers))

    for h in (0, 1):
        mine = ring[h] * 2 + core
        for d in (1, 2, 3):
            for k in (0, 1):
                send(rg, RG.at[h, mine], s_rg_s.at[h], s_rg_r.at[h], dev(h, d, k))
        send(rg, RG.at[h, mine], s_rg_s.at[h], s_rg_r.at[h], dev(h, 0, other))
        copy(rg, RG.at[h, mine], s_rg_r.at[h])

    def gather_start(a):
        for h in (0, 1):
            mine = ring[h] * 2 + core
            for d, k in ((1, 0), (3, 1)):
                for q in (0, 1):
                    send(OWN.at[a, :, :, cols(h, q)], G.at[a, h, mine], s_g_s.at[a, h], s_g_r.at[a, h, k], dev(h, d, q))
            send(OWN.at[a, :, :, cols(h, other)], G.at[a, h, mine], s_g_s.at[a, h], s_g_r.at[a, h, 4], dev(h, 0, other))
            copy(OWN.at[a, :, :, cols(h, core)], G.at[a, h, mine], s_g_r.at[a, h, 5])

    def gather_forward(a):
        for h in (0, 1):
            left = 2 * at(h, 3)
            wait(G.at[a, h, pl.ds(left, 2)], s_g_r.at[a, h, 0])
            for k in (0, 1):
                part = G.at[a, h, left + k, pl.ds(0, 4)]
                send(part, part, s_g_s.at[a, h], s_g_r.at[a, h, 2], dev(h, 1, core))
        for h in (0, 1):
            right = 2 * at(h, 1)
            wait(G.at[a, h, pl.ds(right, 2)], s_g_r.at[a, h, 1])
            for k in (0, 1):
                part = G.at[a, h, right + k, pl.ds(4, 4)]
                send(part, part, s_g_s.at[a, h], s_g_r.at[a, h, 3], dev(h, 3, core))

    def gather_finish(a, h):
        far = 2 * at(h, 2)
        wait(G.at[a, h, pl.ds(far, 2), pl.ds(0, 4)], s_g_r.at[a, h, 2])
        wait(G.at[a, h, pl.ds(far, 2), pl.ds(4, 4)], s_g_r.at[a, h, 3])
        wait(G.at[a, h, ring[h] * 2 + other], s_g_r.at[a, h, 4])
        wait(G.at[a, h, ring[h] * 2 + core], s_g_r.at[a, h, 5])

    def gather_sent(a):
        for h in (0, 1):
            wait(G.at[a, h, pl.ds(0, 7)], s_g_s.at[a, h])

    wait(OWN.at[0], s_o.at[0])
    gather_start(0)
    wait(OWN.at[1], s_o.at[1])
    normalize(1)
    copy(wd, WD, s_w.at[2])
    copy(wg, WG, s_w.at[0])
    copy(wu, WU, s_w.at[1])
    wait(OWN.at[2], s_o.at[2])
    normalize(2)

    def experts(h):
        e = up // 16
        if h == 0:
            ids = (e // 2) * (2 * SIDE) + ring[0] * 2 + e % 2
        else:
            ids = ring[1] * (2 * SIDE) + e
        return ids.astype(F32)

    ids = [experts(h) for h in (0, 1)]
    in_tile = (up % 16).astype(F32)

    def route_row(h, s, row):
        return RG[h, s, pl.ds(row, 1), :]

    def build(st, h):
        def body(s, carry):
            named = (route_row(h, s, 4 * st) == ids[h]) | (route_row(h, s, 4 * st + 1) == ids[h])
            mask = jnp.where(named, 1.0, 0.0)
            before = dot(mask.astype(BF), TRI[...])
            first = 2.0 * s.astype(F32) + in_tile
            PA[st, h, s] = jnp.where(before == first, mask, 0.0).astype(BF)
            PB[st, h, s] = jnp.where(before == first - 16.0, mask, 0.0).astype(BF)
            return carry

        lax.fori_loop(0, 8, body, 0)

    def gates(st, h, s):
        return jnp.where(route_row(h, s, 4 * st) == ids[h], route_row(h, s, 4 * st + 2), route_row(h, s, 4 * st + 3))

    for h in (0, 1):
        wait(RG.at[h], s_rg_r.at[h])
    for h in (0, 1):
        build(1, h)
    gather_start(1)
    for h in (0, 1):
        build(0, h)

    def pack(a, st, h, b, gated):
        def body(i, carry):
            both = rows(G[a, h, pl.ds(i, 2)].reshape(16, 16, QUARTER))
            pick = jnp.concatenate([PA[st, h, i], PB[st, h, i + 1]], axis=1)
            if gated:
                weight = jnp.concatenate([gates(st, h, i), gates(st, h, i + 1)], axis=1)
                high, low = split(pick.astype(F32) * weight)
                out = dot(high, both) + dot(low, both)
            else:
                out = dot(pick, both)
            S[b, h, :, i] = tiles(out.astype(BF))
            return carry

        lax.fori_loop(0, 7, body, 0)

    def scatter_start(a, h, b):
        place_at = pl.ds(7 * ring[1 - h], 7)
        for d in (1, 3, 2):
            for k in (0, 1):
                send(
                    S.at[b, h, 2 * at(1 - h, d) + k, pl.ds(0, 7)], X[h].at[a, place_at, :, qcols(core)],
                    s_x_s.at[a, h], s_x_r.at[a, h], dev(1 - h, d, k),
                )
        send(
            S.at[b, h, 2 * ring[1 - h] + other, pl.ds(0, 7)], X[h].at[a, place_at, :, qcols(core)],
            s_x_s.at[a, h], s_x_r.at[a, h], dev(1 - h, 0, other),
        )
        copy(S.at[b, h, 2 * ring[1 - h] + core, pl.ds(0, 7)], X[h].at[a, place_at, :, qcols(core)], s_l.at[a, h])

    def scatter_sent(a, b):
        for h in (0, 1):
            wait(S.at[b, h, pl.ds(0, 7), pl.ds(0, 7)], s_x_s.at[a, h])
            wait(S.at[b, h, 0, pl.ds(0, 7)], s_l.at[a, h])

    def scatter_finish(a, b):
        for h in (0, 1):
            wait(S.at[b, h, pl.ds(0, 7), pl.ds(0, 7)], s_x_r.at[a, h])

    gather_forward(0)
    for h in (0, 1):

        def turn(s, carry):
            for k, T in enumerate((PB, PA)):
                spot = pl.ds(128 * k, 128)
                PT[h, s, :, spot] = dot_nt(EYE[...], T[1, h, s]).astype(BF)
                for n, part in enumerate(split(T[0, h, s].astype(F32) * gates(0, h, s))):
                    PG[n, h, s, :, spot] = dot_nt(EYE[...], part).astype(BF)
            return carry

        lax.fori_loop(0, 8, turn, 0)

    gather_forward(1)
    gather_start(2)
    for h in (0, 1):
        gather_finish(0, h)
        pack(0, 1, h, 0, True)
        scatter_start(0, h, 0)
    gather_sent(0)
    for h in (0, 1):
        gather_finish(1, h)
        pack(1, 1, h, 1, False)
    gather_forward(2)
    for h in (0, 1):
        scatter_start(1, h, 1)
    gather_sent(1)
    scatter_sent(0, 0)
    for h in (0, 1):
        gather_finish(2, h)
        pack(2, 0, h, 0, False)
    gather_sent(2)
    for h in (0, 1):
        scatter_start(2, h, 0)

    def exchange(a):
        def body(n, carry):
            at_cols = pl.ds(pl.multiple_of(n * 896, 896), 896)
            YB[a, :, :, at_cols] = tiles(dot(PERM[...], rows(YB[a, :, :, at_cols])).astype(BF))
            return carry

        lax.fori_loop(0, HALF // 896, body, 0)

    def exchange_hidden(src, dst):
        def body(n, carry):
            at_cols = pl.ds(pl.multiple_of(n * WIDE, WIDE), WIDE)
            dst[1, :, :, at_cols] = tiles(dot(PERM[...], src[:, at_cols]).astype(BF))
            return carry

        lax.fori_loop(0, FE // WIDE, body, 0)

    scatter_finish(0, 0)
    exchange(0)
    wait(WD, s_w.at[2])

    def early_hidden(f, carry):
        at_cols = pl.ds(pl.multiple_of(f * STEP, STEP), STEP)
        HID[:, at_cols] = dot_nt(rows(XA[0]), WD[at_cols, pl.ds(0, HALF)]) + dot_nt(rows(YB[0]), WD[at_cols, pl.ds(HALF, HALF)])
        return carry

    lax.fori_loop(0, FE // STEP, early_hidden, 0)
    wait(WG, s_w.at[0])
    wait(WU, s_w.at[1])
    scatter_finish(1, 1)
    scatter_sent(1, 1)
    exchange(1)

    def into(a, W, at_cols):
        return dot(rows(XA[a]), W[pl.ds(0, HALF), at_cols]) + dot(rows(YB[a]), W[pl.ds(HALF, HALF), at_cols])

    def backward_hidden(f, carry):
        at_cols = pl.ds(pl.multiple_of(f * STEP, STEP), STEP)
        pre_gate = into(1, WG, at_cols)
        pre_up = into(1, WU, at_cols)
        hidden = HID[:, at_cols]
        sig = 1.0 / (1.0 + jnp.exp(-pre_gate))
        GG[:, at_cols] = (hidden * pre_up * sig * (1.0 + pre_gate * (1.0 - sig))).astype(BF)
        UG[:, at_cols] = (hidden * pre_gate * sig).astype(BF)
        return carry

    lax.fori_loop(0, FE // STEP, backward_hidden, 0)
    exchange_hidden(GG, XA)
    exchange_hidden(UG, YB)

    def return_start(b, ch, h, a, quarters=(0, 1), home=True):
        c0, cw = (0, QUARTER) if b == 0 else CHUNKS[ch]
        mine = 2 * ring[1 - h] + core
        n = b * len(CHUNKS) + ch
        dst = G.at[b, h, pl.ds(0, 7), mine, :, pl.ds(c0, cw)]
        for d in (1, 3, 2):
            for q in quarters:
                send(
                    X[h].at[a, pl.ds(7 * at(1 - h, d), 7), :, qcols(q, c0, cw)], dst,
                    s_r_s.at[n, h], s_r_r.at[n, h], dev(1 - h, d, q),
                )
        if home:
            here = pl.ds(7 * ring[1 - h], 7)
            send(X[h].at[a, here, :, qcols(other, c0, cw)], dst, s_r_s.at[n, h], s_r_r.at[n, h], dev(1 - h, 0, other))
            copy(X[h].at[a, here, :, qcols(core, c0, cw)], dst, s_r_r.at[n, h])

    def backward_out(h, first, last):
        def body(n, carry):
            at_rows = pl.ds(pl.multiple_of(h * HALF + n * STEP, STEP), STEP)
            at_cols = pl.ds(pl.multiple_of(n * STEP, STEP), STEP)
            if h == 0:
                gg, ug = GG[...], UG[...]
            else:
                gg, ug = rows(XA[1, :, :, pl.ds(0, FE)]), rows(YB[1, :, :, pl.ds(0, FE)])
            X[h][0, :, :, at_cols] = tiles((dot_nt(gg, WG[at_rows, :]) + dot_nt(ug, WU[at_rows, :])).astype(BF))
            return carry

        lax.fori_loop(first, last, body, 0)

    for q, first, last in ((0, 0, 4), (1, 4, HALF // STEP)):
        for h in (0, 1):
            backward_out(h, first, last)
        for h in (0, 1):
            return_start(0, 0, h, 0, (q,), q == 1)

    scatter_finish(2, 0)
    scatter_sent(2, 0)
    exchange(2)

    def forward_hidden(f, carry):
        at_cols = pl.ds(pl.multiple_of(f * STEP, STEP), STEP)
        pre_gate = into(2, WG, at_cols)
        pre_up = into(2, WU, at_cols)
        GG[:, at_cols] = (pre_gate * pre_up / (1.0 + jnp.exp(-pre_gate))).astype(BF)
        return carry

    lax.fori_loop(0, FE // STEP, forward_hidden, 0)
    exchange_hidden(GG, XA)
    def forward_out(ch):
        c0, cw = CHUNKS[ch]
        for h in (0, 1):
            for q in (0, 1):
                for n in range(0, cw, STEP):
                    w = min(STEP, cw - n)
                    act = GG[...] if h == 0 else rows(XA[1, :, :, pl.ds(0, FE)])
                    start = q * QUARTER + c0 + n
                    X[h][2, :, :, pl.ds(start, w)] = tiles(dot(act, WD[:, pl.ds(h * HALF + start, w)]).astype(BF))

    def forward_return(ch):
        for h in (0, 1):
            return_start(1, ch, h, 2)

    forward_out(0)
    forward_return(0)

    copy(bin_, OWN.at[1], s_o.at[1])
    copy(fin, OWN.at[2], s_o.at[2])

    def combine(b, ch, h, ds):
        c0, cw = (0, QUARTER) if b == 0 else CHUNKS[ch]
        to = 1 if b == 0 else 0
        here = pl.ds(c0, cw)
        for d in ds:
            for k in (0, 1):
                s = 2 * at(h, d) + k
                prev = rows(G[b, h, jnp.maximum(s - 1, 0), :, :, here])
                cur = rows(G[b, h, jnp.minimum(s, 6), :, :, here])
                both = jnp.concatenate([prev, cur], axis=0)
                if b == 0:
                    out = dot(PT[h, s], both)
                else:
                    out = dot(PG[0, h, s], both) + dot(PG[1, h, s], both)
                S[to, h, s, :, :, here] = tiles(out.astype(BF))

    def land(b):
        return L if b == 0 else G.at[2]

    def meta(b, ch):
        c0, cw = (0, QUARTER) if b == 0 else CHUNKS[ch]
        return b * len(CHUNKS) + ch, pl.ds(c0, cw), (1 if b == 0 else 0), land(b)

    def far_start(b, ch, h):
        n, here, to, B = meta(b, ch)
        far = 2 * at(h, 2)
        combine(b, ch, h, (2,))
        for k in (0, 1):
            send(S.at[to, h, far + k, pl.ds(0, 4), :, here], B.at[h, 6, pl.ds(4 * k, 4), :, here], s_t1_s.at[n, h], s_t1_r.at[n, h, 0], dev(h, 1, core))
            send(S.at[to, h, far + k, pl.ds(4, 4), :, here], B.at[h, 7, pl.ds(4 * k, 4), :, here], s_t1_s.at[n, h], s_t1_r.at[n, h, 1], dev(h, 3, core))

    def own_start(b, ch, h, ds=(1, 3, 0)):
        n, here, to, B = meta(b, ch)
        combine(b, ch, h, ds)
        send(S.at[to, h, 2 * ring[h] + other, :, :, here], B.at[h, 4 + core, :, :, here], s_t2_s.at[n, h], s_c_r.at[n, h, 0], dev(h, 0, other))
        copy(S.at[to, h, 2 * ring[h] + core, :, :, here], B.at[h, 4 + core, :, :, here], s_c_r.at[n, h, 1])

    def near_start(b, ch, h):
        n, here, to, B = meta(b, ch)
        for slot, d, t0, base in ((6, 1, 0, 0), (7, 3, 4, 2)):
            wait(B.at[h, slot, :, :, here], s_t1_r.at[n, h, slot - 6])
            near = 2 * at(h, d)
            for k in (0, 1):
                own = S[to, h, near + k, pl.ds(t0, 4), :, here].astype(F32)
                got = B[h, slot, pl.ds(4 * k, 4), :, here].astype(F32)
                S[to, h, near + k, pl.ds(t0, 4), :, here] = (own + got).astype(BF)
                send(S.at[to, h, near + k, :, :, here], B.at[h, base + core, :, :, here], s_t2_s.at[n, h], s_t2_r.at[n, h], dev(h, d, k))

    def relay_direct(ch):
        n, here, to, B = meta(1, ch)
        for h in (0, 1):
            wait(G.at[1, h, pl.ds(0, 7), :, :, here], s_r_r.at[n, h])
        for d, base in ((2, 6), (1, 0), (3, 2)):
            for h in (0, 1):
                combine(1, ch, h, (d,))
                for k in (0, 1):
                    ss, rs = (s_t1_s.at[n, h], s_t1_r.at[n, h, 0]) if d == 2 else (s_t2_s.at[n, h], s_t2_r.at[n, h])
                    send(S.at[to, h, 2 * at(h, d) + k, :, :, here], B.at[h, base + core, :, :, here], ss, rs, dev(h, d, k))
        for h in (0, 1):
            own_start(1, ch, h, (0,))

    def near_finish(b, ch, h):
        n, here, to, B = meta(b, ch)
        if b == 1 and ch in DIRECT:
            wait(B.at[h, pl.ds(6, 2), :, :, here], s_t1_r.at[n, h, 0])
        wait(B.at[h, pl.ds(0, 4), :, :, here], s_t2_r.at[n, h])
        wait(B.at[h, 4 + other, :, :, here], s_c_r.at[n, h, 0])
        wait(B.at[h, 4 + core, :, :, here], s_c_r.at[n, h, 1])

    def arrived(b, h, q, k, here, direct=False):
        B = land(b)
        far = B[h, 6 + q, k, :, here].astype(F32) if direct else 0.0
        return far + B[h, q, k, :, here].astype(F32) + B[h, 2 + q, k, :, here].astype(F32) + B[h, 4 + q, k, :, here].astype(F32)

    for h in (0, 1):
        wait(G.at[0, h, pl.ds(0, 7)], s_r_r.at[0, h])
        far_start(0, 0, h)
    for h in (0, 1):
        own_start(0, 0, h)
    def relay_far(ch):
        n, here, to, B = meta(1, ch)
        for h in (0, 1):
            wait(G.at[1, h, pl.ds(0, 7), :, :, here], s_r_r.at[n, h])
            far_start(1, ch, h)
        for h in (0, 1):
            own_start(1, ch, h)

    def relay_near(ch):
        for h in (0, 1):
            near_start(1, ch, h)

    forward_out(1)
    relay_far(0)
    forward_return(1)
    forward_out(2)
    forward_out(3)
    relay_near(0)
    for h in (0, 1):
        near_start(0, 0, h)
    relay_far(1)
    forward_return(2)
    forward_return(3)

    def forward_last(ch):
        c0, cw = CHUNKS[ch]
        n, here, to, B = meta(1, ch)
        for h in (0, 1):
            near_finish(1, ch, h)

            def body(k, carry):
                for q in (0, 1):
                    spot = pl.ds(h * HALF + q * QUARTER + c0, cw)
                    OWN[2, k, :, spot] = (OWN[2, k, :, spot].astype(F32) + arrived(1, h, q, k, here, ch in DIRECT)).astype(BF)
                return carry

            lax.fori_loop(0, 8, body, 0)
            for q in (0, 1):
                spot = pl.ds(h * HALF + q * QUARTER + c0, cw)
                send(OWN.at[2, :, :, spot], fo.at[:, :, spot], s_y_s.at[1 + ch], s_y_r.at[1 + ch], ahead)

    wait(OWN.at[1], s_o.at[1])
    wait(OWN.at[2], s_o.at[2])
    forward_last(0)
    for h in (0, 1):
        near_finish(0, 0, h)

    def backward_last(k, carry):
        summed = jnp.concatenate([arrived(0, h, q, k, pl.ds(0, QUARTER)) for h in (0, 1) for q in (0, 1)], axis=1)
        stored = OWN[1, k].astype(F32)
        r = lax.rsqrt(jnp.mean(stored * stored, axis=-1, keepdims=True) + EPSILON)
        grad = gain[...].astype(F32) * summed
        mean = jnp.mean(stored * grad, axis=-1, keepdims=True)
        OWN[1, k] = (OWN[0, k].astype(F32) + r * grad - stored * (r * r * r) * mean).astype(BF)
        return carry

    for first in (0, 4):
        lax.fori_loop(first, first + 4, backward_last, 0)
        part = pl.ds(first, 4)
        send(OWN.at[1, part], bo.at[part], s_y_s.at[0], s_y_r.at[0], behind)

    relay_near(1)
    relay_direct(2)
    forward_last(1)
    relay_direct(3)
    forward_last(2)
    forward_last(3)

    for h in (0, 1):
        wait(RG.at[h, pl.ds(0, 7)], s_rg_s.at[h])
    for b, chunks in ((0, ((0, QUARTER),)), (1, CHUNKS)):
        for ch, (c0, cw) in enumerate(chunks):
            n, here, to, B = meta(b, ch)
            for h in (0, 1):
                wait(S.at[to, h, pl.ds(0, 7), pl.ds(0, 7), :, here], s_r_s.at[n, h])
                wait(S.at[to, h, pl.ds(0, 2), :, :, here], s_t1_s.at[n, h])
                wait(S.at[to, h, pl.ds(0, 5), :, :, here], s_t2_s.at[n, h])
    wait(bo, s_y_s.at[0])
    wait(bo, s_y_r.at[0])
    for ch, (c0, cw) in enumerate(CHUNKS):
        wait(fo.at[:, :, pl.ds(0, 4 * cw)], s_y_s.at[1 + ch])
        wait(fo.at[:, :, pl.ds(0, 4 * cw)], s_y_r.at[1 + ch])


def hand_over(fo, bo, f_out, b_out, held, sem):
    parts = [(i, pl.ds(4 * k, 4)) for i in (0, 1) for k in (0, 1)]
    loads = [pltpu.make_async_copy((fo, bo)[i].at[at], held.at[i, at], sem.at[0, n]) for n, (i, at) in enumerate(parts)]
    stores = [pltpu.make_async_copy(held.at[i, at], (f_out, b_out)[i].at[at], sem.at[1, n]) for n, (i, at) in enumerate(parts)]
    for copy in loads:
        copy.start()
    for load, store in zip(loads, stores):
        load.wait()
        store.start()
    for copy in stores:
        copy.wait()


def local(
    forward_input,
    forward_routes,
    forward_gates,
    backward_input,
    backward_routes,
    backward_gates,
    upstream_gradient,
    norm_gain,
    gate_weight,
    up_weight,
    down_weight,
):
    shape = (8, 16, D)
    parts = 1 + len(CHUNKS)
    groups = 2 * len(CHUNKS)
    dma = pltpu.SemaphoreType.DMA
    vmem = pl.BlockSpec(memory_space=pltpu.VMEM)
    anywhere = pl.BlockSpec(memory_space=pl.ANY)
    fo, bo = pl.pallas_call(
        kernel,
        name="relay",
        out_shape=(jax.ShapeDtypeStruct(shape, BF), jax.ShapeDtypeStruct(shape, BF)),
        in_specs=[vmem] * 4 + [anywhere] * 3 + [vmem] + [anywhere] * 3,
        out_specs=(anywhere, anywhere),
        scratch_shapes=[
            pltpu.VMEM((D, FE), BF),
            pltpu.VMEM((D, FE), BF),
            pltpu.VMEM((FE, D), BF),
            pltpu.VMEM((3, 2, 8, 8, 16, QUARTER), BF),
            pltpu.VMEM((3, 28, 16, HALF), BF),
            pltpu.VMEM((3, 28, 16, HALF), BF),
            pltpu.VMEM((2, 2, 8, 8, 16, QUARTER), BF),
            pltpu.VMEM((2, 8, 8, 16, QUARTER), BF),
            pltpu.VMEM((3, 8, 16, D), BF),
            pltpu.VMEM((2, 8, 8, 128), F32),
            pltpu.VMEM((2, 2, 8, 128, 128), BF),
            pltpu.VMEM((2, 2, 8, 128, 128), BF),
            pltpu.VMEM((448, FE), BF),
            pltpu.VMEM((448, FE), BF),
            pltpu.VMEM((448, FE), F32),
            pltpu.VMEM((448, 448), BF),
            pltpu.VMEM((128, 128), BF),
            pltpu.VMEM((128, 128), BF),
            pltpu.VMEM((2, 8, 128, 256), BF),
            pltpu.VMEM((2, 2, 8, 128, 256), BF),
            pltpu.VMEM((8, 128), F32),
            dma((2,)),
            dma((2,)),
            dma((3, 2, 6)),
            dma((3, 2)),
            dma((3, 2)),
            dma((3, 2)),
            dma((groups, 2)),
            dma((groups, 2)),
            dma((groups, 2, 2)),
            dma((groups, 2)),
            dma((groups, 2)),
            dma((groups, 2)),
            dma((groups, 2, 2)),
            dma((parts,)),
            dma((parts,)),
            dma((3,)),
            dma((3,)),
            dma((3, 2)),
        ],
        compiler_params=pltpu.CompilerParams(
            collective_id=0, has_side_effects=True, vmem_limit_bytes=64 * 1024 * 1024 - 65536
        ),
        cost_estimate=pl.CostEstimate(flops=46 * 10**9, bytes_accessed=30 * 10**6, transcendentals=10**6),
    )(
        forward_routes[0].T,
        forward_gates[0].T,
        backward_routes[0].T,
        backward_gates[0].T,
        forward_input.reshape(shape),
        backward_input.reshape(shape),
        upstream_gradient.reshape(shape),
        norm_gain,
        gate_weight[0, 0],
        up_weight[0, 0],
        down_weight[0, 0],
    )
    fo, bo = pl.pallas_call(
        hand_over,
        name="results",
        out_shape=(jax.ShapeDtypeStruct(shape, BF), jax.ShapeDtypeStruct(shape, BF)),
        in_specs=[anywhere] * 2,
        out_specs=(anywhere, anywhere),
        scratch_shapes=[pltpu.VMEM((2,) + shape, BF), dma((2, 4))],
        cost_estimate=pl.CostEstimate(flops=0, bytes_accessed=4 * 10**6, transcendentals=0),
    )(fo, bo)
    return (fo.reshape(1, 128, D), bo.reshape(1, 128, D))


def solution(mesh):
    rows_spec = P("pipe", "expert", None)
    weight = P("pipe", "expert", None, None)
    in_specs = (rows_spec,) * 7 + (P("pipe", None), weight, weight, weight)
    out_specs = (rows_spec, rows_spec)
    return jax.shard_map(local, mesh=mesh, in_specs=in_specs, out_specs=out_specs, check_vma=False)
```

```python
import functools

import jax
import jax.numpy as jnp
from jax import lax
from jax.experimental import pallas as pl
from jax.experimental.pallas import tpu as pltpu
from jax.sharding import PartitionSpec as P

EPSILON = 1e-06
MESH = pl.DeviceIdType.MESH
BF = jnp.bfloat16
F32 = jnp.float32
D = 3584
FE = 1024
HALF = D // 2
QUARTER = D // 4
SIDE = 4
SLOTS = 14
CHUNKS = ((0, 384), (384, 256), (640, 128), (768, 128))
DIRECT = (2, 3)
PARTS = ((0, 3), (3, 1))
STEP = 256
WIDE = 512


def dot(a, b):
    return jnp.dot(a, b, preferred_element_type=F32)


def dot_nt(a, b):
    return lax.dot_general(a, b, (((1,), (1,)), ((), ())), preferred_element_type=F32)


def rows(value):
    return value.reshape(value.shape[-3] * value.shape[-2], value.shape[-1])


def tiles(value):
    return value.reshape(value.shape[0] // 16, 16, value.shape[1])


def split(value):
    high = value.astype(BF)
    return high, (value - high.astype(F32)).astype(BF)


def kernel(
    fr_in, fg_in, br_in, bg_in, fin, bin_, upg, gain_in, wg, wu, wd, fo, bo,
    WG, WU, WD, G, XA, YB, S, L, OWN, RG, PA, PB, GG, UG, HID, PERM, PT, PG, rg, fr, fg, br, bg, gain,
    s_rg_r, s_rg_s, s_g_r, s_g_s, s_x_r, s_x_s, s_r_r, s_r_s,
    s_t1_r, s_t1_s, s_t2_r, s_t2_s, s_c_r, s_y_r, s_y_s, s_w, s_o, s_l, s_i,
):
    pipe = lax.axis_index("pipe")
    me = lax.axis_index("expert")
    core = lax.rem(me, 2)
    other = 1 - core
    ring = (lax.rem(me // 2, SIDE), me // (2 * SIDE))
    X = (XA, YB)

    def at(h, delta):
        return lax.rem(ring[h] + delta, SIDE)

    def dev(h, delta, k):
        r = at(h, delta)
        if h == 0:
            return (pipe, (ring[1] * SIDE + r) * 2 + k)
        return (pipe, (r * SIDE + ring[0]) * 2 + k)

    def cols(h, q, c0=0, cw=QUARTER):
        return pl.ds(pl.multiple_of(h * HALF + q * QUARTER + c0, 128), cw)

    def qcols(q, c0=0, cw=QUARTER):
        return pl.ds(pl.multiple_of(q * QUARTER + c0, 128), cw)

    def send(src, dst, ss, rs, device):
        pltpu.make_async_remote_copy(
            src_ref=src, dst_ref=dst, send_sem=ss, recv_sem=rs, device_id=device, device_id_type=MESH
        ).start()

    def copy(src, dst, sem):
        pltpu.make_async_copy(src, dst, sem).start()

    def wait(ref, sem):
        pltpu.make_async_copy(ref, ref, sem).wait()

    barrier = pltpu.get_barrier_semaphore()
    peers = [dev(h, d, k) for h in (0, 1) for d in (1, 2, 3) for k in (0, 1)]
    peers.append(dev(0, 0, other))
    ahead = (lax.rem(pipe + 1, SIDE), me)
    behind = (lax.rem(pipe + 3, SIDE), me)
    peers += [ahead, behind]
    for peer in peers:
        pl.semaphore_signal(barrier, inc=1, device_id=peer, device_id_type=MESH)
    def normalize(a):
        def body(k, carry):
            v = OWN[a, k].astype(F32)
            r = lax.rsqrt(jnp.mean(v * v, axis=-1, keepdims=True) + EPSILON)
            OWN[a, k] = (v * r * gain[...].astype(F32)).astype(BF)
            return carry

        lax.fori_loop(0, 8, body, 0)

    copy(upg, OWN.at[0], s_o.at[0])
    copy(bin_, OWN.at[1], s_o.at[1])
    copy(fin, OWN.at[2], s_o.at[2])

    small = ((fr_in, fr), (fg_in, fg), (br_in, br), (bg_in, bg), (gain_in, gain))
    for n, (src, dst) in enumerate(small):
        copy(src, dst, s_i.at[n])
    for n, (src, dst) in enumerate(small):
        wait(dst, s_i.at[n])
    rg[pl.ds(0, 2), :] = fr[...].astype(F32)
    rg[pl.ds(2, 2), :] = fg[...]
    rg[pl.ds(4, 2), :] = br[...].astype(F32)
    rg[pl.ds(6, 2), :] = bg[...]

    up = lax.broadcasted_iota(jnp.int32, (128, 128), 0)
    across = lax.broadcasted_iota(jnp.int32, (128, 128), 1)
    triangle = jnp.where(up < across, 1.0, 0.0).astype(BF)
    identity = jnp.where(up == across, 1.0, 0.0).astype(BF)
    line = lax.broadcasted_iota(jnp.int32, (448, 448), 0)
    outer = (line >= 112).astype(jnp.int32) + (line >= 224).astype(jnp.int32) + (line >= 336).astype(jnp.int32)
    rest = line - 112 * outer
    inner = (rest >= 28).astype(jnp.int32) + (rest >= 56).astype(jnp.int32) + (rest >= 84).astype(jnp.int32)
    place = 112 * inner + 28 * outer + rest - 28 * inner
    PERM[...] = jnp.where(lax.broadcasted_iota(jnp.int32, (448, 448), 1) == place, 1.0, 0.0).astype(BF)

    pl.semaphore_wait(barrier, len(peers))

    for h in (0, 1):
        mine = ring[h] * 2 + core
        for d in (1, 2, 3):
            for k in (0, 1):
                send(rg, RG.at[h, mine], s_rg_s.at[h], s_rg_r.at[h], dev(h, d, k))
        send(rg, RG.at[h, mine], s_rg_s.at[h], s_rg_r.at[h], dev(h, 0, other))
        copy(rg, RG.at[h, mine], s_rg_r.at[h])

    def gather_start(a):
        for h in (0, 1):
            mine = ring[h] * 2 + core
            for d, k in ((1, 0), (3, 1)):
                for q in (0, 1):
                    send(OWN.at[a, :, :, cols(h, q)], G.at[a, h, mine], s_g_s.at[a, h], s_g_r.at[a, h, k], dev(h, d, q))
            send(OWN.at[a, :, :, cols(h, other)], G.at[a, h, mine], s_g_s.at[a, h], s_g_r.at[a, h, 4], dev(h, 0, other))
            copy(OWN.at[a, :, :, cols(h, core)], G.at[a, h, mine], s_g_r.at[a, h, 5])

    def gather_forward(a):
        for h in (0, 1):
            left = 2 * at(h, 3)
            wait(G.at[a, h, pl.ds(left, 2)], s_g_r.at[a, h, 0])
            for k in (0, 1):
                part = G.at[a, h, left + k, pl.ds(0, 4)]
                send(part, part, s_g_s.at[a, h], s_g_r.at[a, h, 2], dev(h, 1, core))
        for h in (0, 1):
            right = 2 * at(h, 1)
            wait(G.at[a, h, pl.ds(right, 2)], s_g_r.at[a, h, 1])
            for k in (0, 1):
                part = G.at[a, h, right + k, pl.ds(4, 4)]
                send(part, part, s_g_s.at[a, h], s_g_r.at[a, h, 3], dev(h, 3, core))

    def gather_finish(a, h):
        far = 2 * at(h, 2)
        wait(G.at[a, h, pl.ds(far, 2), pl.ds(0, 4)], s_g_r.at[a, h, 2])
        wait(G.at[a, h, pl.ds(far, 2), pl.ds(4, 4)], s_g_r.at[a, h, 3])
        wait(G.at[a, h, ring[h] * 2 + other], s_g_r.at[a, h, 4])
        wait(G.at[a, h, ring[h] * 2 + core], s_g_r.at[a, h, 5])

    def gather_sent(a):
        for h in (0, 1):
            wait(G.at[a, h, pl.ds(0, 7)], s_g_s.at[a, h])

    wait(OWN.at[0], s_o.at[0])
    gather_start(0)
    wait(OWN.at[1], s_o.at[1])
    normalize(1)
    copy(wd, WD, s_w.at[2])
    copy(wg, WG, s_w.at[0])
    copy(wu, WU, s_w.at[1])
    wait(OWN.at[2], s_o.at[2])
    normalize(2)

    def experts(h):
        e = up // 16
        if h == 0:
            ids = (e // 2) * (2 * SIDE) + ring[0] * 2 + e % 2
        else:
            ids = ring[1] * (2 * SIDE) + e
        return ids.astype(F32)

    ids = [experts(h) for h in (0, 1)]
    in_tile = (up % 16).astype(F32)

    def route_row(h, s, row):
        return RG[h, s, pl.ds(row, 1), :]

    def build(st, h):
        def body(s, carry):
            named = (route_row(h, s, 4 * st) == ids[h]) | (route_row(h, s, 4 * st + 1) == ids[h])
            mask = jnp.where(named, 1.0, 0.0)
            before = dot(mask.astype(BF), triangle)
            first = 2.0 * s.astype(F32) + in_tile
            PA[st, h, s] = jnp.where(before == first, mask, 0.0).astype(BF)
            PB[st, h, s] = jnp.where(before == first - 16.0, mask, 0.0).astype(BF)
            return carry

        lax.fori_loop(0, 8, body, 0)

    def gates(st, h, s):
        return jnp.where(route_row(h, s, 4 * st) == ids[h], route_row(h, s, 4 * st + 2), route_row(h, s, 4 * st + 3))

    for h in (0, 1):
        wait(RG.at[h], s_rg_r.at[h])
    for h in (0, 1):
        build(1, h)
    gather_start(1)
    for h in (0, 1):
        build(0, h)

    def pack(a, st, h, b, gated):
        def body(i, carry):
            both = rows(G[a, h, pl.ds(i, 2)].reshape(16, 16, QUARTER))
            pick = jnp.concatenate([PA[st, h, i], PB[st, h, i + 1]], axis=1)
            if gated:
                weight = jnp.concatenate([gates(st, h, i), gates(st, h, i + 1)], axis=1)
                high, low = split(pick.astype(F32) * weight)
                out = dot(high, both) + dot(low, both)
            else:
                out = dot(pick, both)
            S[b, h, :, i] = tiles(out.astype(BF))
            return carry

        lax.fori_loop(0, 7, body, 0)

    def scatter_start(a, h, b):
        place_at = pl.ds(7 * ring[1 - h], 7)
        for d in (1, 3, 2):
            for k in (0, 1):
                send(
                    S.at[b, h, 2 * at(1 - h, d) + k, pl.ds(0, 7)], X[h].at[a, place_at, :, qcols(core)],
                    s_x_s.at[a, h], s_x_r.at[a, h], dev(1 - h, d, k),
                )
        send(
            S.at[b, h, 2 * ring[1 - h] + other, pl.ds(0, 7)], X[h].at[a, place_at, :, qcols(core)],
            s_x_s.at[a, h], s_x_r.at[a, h], dev(1 - h, 0, other),
        )
        copy(S.at[b, h, 2 * ring[1 - h] + core, pl.ds(0, 7)], X[h].at[a, place_at, :, qcols(core)], s_l.at[a, h])

    def scatter_sent(a, b):
        for h in (0, 1):
            wait(S.at[b, h, pl.ds(0, 7), pl.ds(0, 7)], s_x_s.at[a, h])
            wait(S.at[b, h, 0, pl.ds(0, 7)], s_l.at[a, h])

    def scatter_finish(a, b):
        for h in (0, 1):
            wait(S.at[b, h, pl.ds(0, 7), pl.ds(0, 7)], s_x_r.at[a, h])

    gather_forward(0)
    for h in (0, 1):

        def turn(s, carry):
            for k, T in enumerate((PB, PA)):
                spot = pl.ds(128 * k, 128)
                PT[h, s, :, spot] = dot_nt(identity, T[1, h, s]).astype(BF)
                for n, part in enumerate(split(T[0, h, s].astype(F32) * gates(0, h, s))):
                    PG[n, h, s, :, spot] = dot_nt(identity, part).astype(BF)
            return carry

        lax.fori_loop(0, 8, turn, 0)

    gather_forward(1)
    gather_start(2)
    for h in (0, 1):
        gather_finish(0, h)
        pack(0, 1, h, 0, True)
        scatter_start(0, h, 0)
    gather_sent(0)
    for h in (0, 1):
        gather_finish(1, h)
        pack(1, 1, h, 1, False)
    gather_forward(2)
    for h in (0, 1):
        scatter_start(1, h, 1)
    gather_sent(1)
    scatter_sent(0, 0)
    for h in (0, 1):
        gather_finish(2, h)
        pack(2, 0, h, 0, False)
    gather_sent(2)
    for h in (0, 1):
        scatter_start(2, h, 0)

    def exchange(a):
        def body(n, carry):
            at_cols = pl.ds(pl.multiple_of(n * 896, 896), 896)
            YB[a, :, :, at_cols] = tiles(dot(PERM[...], rows(YB[a, :, :, at_cols])).astype(BF))
            return carry

        lax.fori_loop(0, HALF // 896, body, 0)

    def exchange_hidden(src, dst):
        def body(n, carry):
            at_cols = pl.ds(pl.multiple_of(n * WIDE, WIDE), WIDE)
            dst[1, :, :, at_cols] = tiles(dot(PERM[...], src[:, at_cols]).astype(BF))
            return carry

        lax.fori_loop(0, FE // WIDE, body, 0)

    scatter_finish(0, 0)
    exchange(0)
    wait(WD, s_w.at[2])

    def early_hidden(f, carry):
        at_cols = pl.ds(pl.multiple_of(f * STEP, STEP), STEP)
        HID[:, at_cols] = dot_nt(rows(XA[0]), WD[at_cols, pl.ds(0, HALF)]) + dot_nt(rows(YB[0]), WD[at_cols, pl.ds(HALF, HALF)])
        return carry

    lax.fori_loop(0, FE // STEP, early_hidden, 0)
    wait(WG, s_w.at[0])
    wait(WU, s_w.at[1])
    scatter_finish(1, 1)
    scatter_sent(1, 1)
    exchange(1)

    def into(a, W, at_cols):
        return dot(rows(XA[a]), W[pl.ds(0, HALF), at_cols]) + dot(rows(YB[a]), W[pl.ds(HALF, HALF), at_cols])

    def backward_hidden(f, carry):
        at_cols = pl.ds(pl.multiple_of(f * STEP, STEP), STEP)
        pre_gate = into(1, WG, at_cols)
        pre_up = into(1, WU, at_cols)
        hidden = HID[:, at_cols]
        sig = 1.0 / (1.0 + jnp.exp(-pre_gate))
        GG[:, at_cols] = (hidden * pre_up * sig * (1.0 + pre_gate * (1.0 - sig))).astype(BF)
        UG[:, at_cols] = (hidden * pre_gate * sig).astype(BF)
        return carry

    lax.fori_loop(0, FE // STEP, backward_hidden, 0)
    exchange_hidden(GG, XA)
    exchange_hidden(UG, YB)

    def return_start(b, ch, h, a, quarters=(0, 1), home=True):
        c0, cw = (0, QUARTER) if b == 0 else CHUNKS[ch]
        mine = 2 * ring[1 - h] + core
        n = b * len(CHUNKS) + ch
        dst = G.at[b, h, pl.ds(0, 7), mine, :, pl.ds(c0, cw)]
        for d in (1, 3, 2):
            for q in quarters:
                send(
                    X[h].at[a, pl.ds(7 * at(1 - h, d), 7), :, qcols(q, c0, cw)], dst,
                    s_r_s.at[n, h], s_r_r.at[n, h], dev(1 - h, d, q),
                )
        if home:
            here = pl.ds(7 * ring[1 - h], 7)
            send(X[h].at[a, here, :, qcols(other, c0, cw)], dst, s_r_s.at[n, h], s_r_r.at[n, h], dev(1 - h, 0, other))
            copy(X[h].at[a, here, :, qcols(core, c0, cw)], dst, s_r_r.at[n, h])

    def backward_out(h, first, last):
        def body(n, carry):
            at_rows = pl.ds(pl.multiple_of(h * HALF + n * STEP, STEP), STEP)
            at_cols = pl.ds(pl.multiple_of(n * STEP, STEP), STEP)
            if h == 0:
                gg, ug = GG[...], UG[...]
            else:
                gg, ug = rows(XA[1, :, :, pl.ds(0, FE)]), rows(YB[1, :, :, pl.ds(0, FE)])
            X[h][0, :, :, at_cols] = tiles((dot_nt(gg, WG[at_rows, :]) + dot_nt(ug, WU[at_rows, :])).astype(BF))
            return carry

        lax.fori_loop(first, last, body, 0)

    for q, first, last in ((0, 0, 4), (1, 4, HALF // STEP)):
        for h in (0, 1):
            backward_out(h, first, last)
        for h in (0, 1):
            return_start(0, 0, h, 0, (q,), q == 1)

    scatter_finish(2, 0)
    scatter_sent(2, 0)
    exchange(2)

    def forward_hidden(f, carry):
        at_cols = pl.ds(pl.multiple_of(f * STEP, STEP), STEP)
        pre_gate = into(2, WG, at_cols)
        pre_up = into(2, WU, at_cols)
        GG[:, at_cols] = (pre_gate * pre_up / (1.0 + jnp.exp(-pre_gate))).astype(BF)
        return carry

    lax.fori_loop(0, FE // STEP, forward_hidden, 0)
    exchange_hidden(GG, XA)
    def forward_out(ch):
        c0, cw = CHUNKS[ch]
        for h in (0, 1):
            for q in (0, 1):
                for n in range(0, cw, STEP):
                    w = min(STEP, cw - n)
                    act = GG[...] if h == 0 else rows(XA[1, :, :, pl.ds(0, FE)])
                    start = q * QUARTER + c0 + n
                    X[h][2, :, :, pl.ds(start, w)] = tiles(dot(act, WD[:, pl.ds(h * HALF + start, w)]).astype(BF))

    def forward_return(ch):
        for h in (0, 1):
            return_start(1, ch, h, 2)

    forward_out(0)
    forward_return(0)

    copy(bin_, OWN.at[1], s_o.at[1])
    copy(fin, OWN.at[2], s_o.at[2])

    def combine(b, ch, h, ds):
        c0, cw = (0, QUARTER) if b == 0 else CHUNKS[ch]
        to = 1 if b == 0 else 0
        here = pl.ds(c0, cw)
        for d in ds:
            for k in (0, 1):
                s = 2 * at(h, d) + k
                prev = rows(G[b, h, jnp.maximum(s - 1, 0), :, :, here])
                cur = rows(G[b, h, jnp.minimum(s, 6), :, :, here])
                both = jnp.concatenate([prev, cur], axis=0)
                if b == 0:
                    out = dot(PT[h, s], both)
                else:
                    out = dot(PG[0, h, s], both) + dot(PG[1, h, s], both)
                S[to, h, s, :, :, here] = tiles(out.astype(BF))

    def land(b):
        return L if b == 0 else G.at[2]

    def meta(b, ch):
        c0, cw = (0, QUARTER) if b == 0 else CHUNKS[ch]
        return b * len(CHUNKS) + ch, pl.ds(c0, cw), (1 if b == 0 else 0), land(b)

    def far_start(b, ch, h):
        n, here, to, B = meta(b, ch)
        far = 2 * at(h, 2)
        combine(b, ch, h, (2,))
        for k in (0, 1):
            send(S.at[to, h, far + k, pl.ds(0, 4), :, here], B.at[h, 6, pl.ds(4 * k, 4), :, here], s_t1_s.at[n, h], s_t1_r.at[n, h, 0], dev(h, 1, core))
            send(S.at[to, h, far + k, pl.ds(4, 4), :, here], B.at[h, 7, pl.ds(4 * k, 4), :, here], s_t1_s.at[n, h], s_t1_r.at[n, h, 1], dev(h, 3, core))

    def own_start(b, ch, h, ds=(1, 3, 0)):
        n, here, to, B = meta(b, ch)
        combine(b, ch, h, ds)
        send(S.at[to, h, 2 * ring[h] + other, :, :, here], B.at[h, 4 + core, :, :, here], s_t2_s.at[n, h], s_c_r.at[n, h, 0], dev(h, 0, other))
        copy(S.at[to, h, 2 * ring[h] + core, :, :, here], B.at[h, 4 + core, :, :, here], s_c_r.at[n, h, 1])

    def near_start(b, ch, h):
        n, here, to, B = meta(b, ch)
        for slot, d, t0, base in ((6, 1, 0, 0), (7, 3, 4, 2)):
            wait(B.at[h, slot, :, :, here], s_t1_r.at[n, h, slot - 6])
            near = 2 * at(h, d)
            for k in (0, 1):
                own = S[to, h, near + k, pl.ds(t0, 4), :, here].astype(F32)
                got = B[h, slot, pl.ds(4 * k, 4), :, here].astype(F32)
                S[to, h, near + k, pl.ds(t0, 4), :, here] = (own + got).astype(BF)
                send(S.at[to, h, near + k, :, :, here], B.at[h, base + core, :, :, here], s_t2_s.at[n, h], s_t2_r.at[n, h], dev(h, d, k))

    def stored_near(part):
        n, here, to, B = meta(0, 0)
        start, size = PARTS[part]
        for h in (0, 1):
            for slot, d, t0, base in ((6, 1, 0, 0), (7, 3, 4, 2)):
                if part == 0:
                    wait(B.at[h, slot], s_t1_r.at[n, h, slot - 6])
                near = 2 * at(h, d)
                for k in (0, 1):
                    first = pl.ds(t0 + start, size)
                    own = S[to, h, near + k, first].astype(F32)
                    got = B[h, slot, pl.ds(4 * k + start, size)].astype(F32)
                    S[to, h, near + k, first] = (own + got).astype(BF)
                    for t in (0, 4):
                        both = pl.ds(t + start, size)
                        send(S.at[to, h, near + k, both], B.at[h, base + core, both], s_t2_s.at[part, h], s_t2_r.at[part, h], dev(h, d, k))

    def stored_finish(part):
        n, here, to, B = meta(0, 0)
        for h in (0, 1):
            wait(B.at[h, pl.ds(0, PARTS[part][1])], s_t2_r.at[part, h])
            if part == 0:
                wait(B.at[h, 4 + other], s_c_r.at[n, h, 0])
                wait(B.at[h, 4 + core], s_c_r.at[n, h, 1])

    def relay_direct(ch):
        n, here, to, B = meta(1, ch)
        for h in (0, 1):
            wait(G.at[1, h, pl.ds(0, 7), :, :, here], s_r_r.at[n, h])
        for d, base in ((2, 6), (1, 0), (3, 2)):
            for h in (0, 1):
                combine(1, ch, h, (d,))
                for k in (0, 1):
                    ss, rs = (s_t1_s.at[n, h], s_t1_r.at[n, h, 0]) if d == 2 else (s_t2_s.at[n, h], s_t2_r.at[n, h])
                    send(S.at[to, h, 2 * at(h, d) + k, :, :, here], B.at[h, base + core, :, :, here], ss, rs, dev(h, d, k))
        for h in (0, 1):
            own_start(1, ch, h, (0,))

    def near_finish(b, ch, h):
        n, here, to, B = meta(b, ch)
        if b == 1 and ch in DIRECT:
            wait(B.at[h, pl.ds(6, 2), :, :, here], s_t1_r.at[n, h, 0])
        wait(B.at[h, pl.ds(0, 4), :, :, here], s_t2_r.at[n, h])
        wait(B.at[h, 4 + other, :, :, here], s_c_r.at[n, h, 0])
        wait(B.at[h, 4 + core, :, :, here], s_c_r.at[n, h, 1])

    def arrived(b, h, q, k, here, direct=False):
        B = land(b)
        far = B[h, 6 + q, k, :, here].astype(F32) if direct else 0.0
        return far + B[h, q, k, :, here].astype(F32) + B[h, 2 + q, k, :, here].astype(F32) + B[h, 4 + q, k, :, here].astype(F32)

    for h in (0, 1):
        wait(G.at[0, h, pl.ds(0, 7)], s_r_r.at[0, h])
        far_start(0, 0, h)
    for h in (0, 1):
        own_start(0, 0, h)
    def relay_far(ch):
        n, here, to, B = meta(1, ch)
        for h in (0, 1):
            wait(G.at[1, h, pl.ds(0, 7), :, :, here], s_r_r.at[n, h])
            far_start(1, ch, h)
        for h in (0, 1):
            own_start(1, ch, h)

    def relay_near(ch):
        for h in (0, 1):
            near_start(1, ch, h)

    forward_out(1)
    relay_far(0)
    forward_return(1)
    forward_out(2)
    forward_out(3)
    stored_near(0)
    relay_near(0)
    relay_far(1)
    forward_return(2)

    def forward_last(ch):
        c0, cw = CHUNKS[ch]
        n, here, to, B = meta(1, ch)
        for h in (0, 1):
            near_finish(1, ch, h)

            def body(k, carry):
                for q in (0, 1):
                    spot = pl.ds(h * HALF + q * QUARTER + c0, cw)
                    OWN[2, k, :, spot] = (OWN[2, k, :, spot].astype(F32) + arrived(1, h, q, k, here, ch in DIRECT)).astype(BF)
                return carry

            lax.fori_loop(0, 8, body, 0)
            for q in (0, 1):
                spot = pl.ds(h * HALF + q * QUARTER + c0, cw)
                send(OWN.at[2, :, :, spot], fo.at[:, :, spot], s_y_s.at[1 + ch], s_y_r.at[1 + ch], ahead)

    def backward_last(k, carry):
        summed = jnp.concatenate([arrived(0, h, q, k, pl.ds(0, QUARTER)) for h in (0, 1) for q in (0, 1)], axis=1)
        stored = OWN[1, k].astype(F32)
        r = lax.rsqrt(jnp.mean(stored * stored, axis=-1, keepdims=True) + EPSILON)
        grad = gain[...].astype(F32) * summed
        mean = jnp.mean(stored * grad, axis=-1, keepdims=True)
        OWN[1, k] = (OWN[0, k].astype(F32) + r * grad - stored * (r * r * r) * mean).astype(BF)
        return carry

    def stored_last(part):
        stored_finish(part)
        start, size = PARTS[part]
        for first in (start, 4 + start):
            lax.fori_loop(first, first + size, backward_last, 0)
            both = pl.ds(first, size)
            send(OWN.at[1, both], bo.at[both], s_y_s.at[0], s_y_r.at[0], behind)

    wait(OWN.at[1], s_o.at[1])
    wait(OWN.at[2], s_o.at[2])
    stored_last(0)
    forward_last(0)
    relay_near(1)
    forward_return(3)
    stored_near(1)
    relay_direct(2)
    forward_last(1)
    relay_direct(3)
    stored_last(1)
    forward_last(2)
    forward_last(3)

    for h in (0, 1):
        wait(RG.at[h, pl.ds(0, 7)], s_rg_s.at[h])
    for b, chunks in ((0, ((0, QUARTER),)), (1, CHUNKS)):
        for ch, (c0, cw) in enumerate(chunks):
            n, here, to, B = meta(b, ch)
            for h in (0, 1):
                wait(S.at[to, h, pl.ds(0, 7), pl.ds(0, 7), :, here], s_r_s.at[n, h])
                wait(S.at[to, h, pl.ds(0, 2), :, :, here], s_t1_s.at[n, h])
                wait(S.at[to, h, pl.ds(0, 5 if b == 1 else 1 + PARTS[0][1]), :, :, here], s_t2_s.at[n, h])
                if b == 0:
                    wait(S.at[to, h, pl.ds(0, PARTS[1][1])], s_t2_s.at[1, h])
    wait(bo, s_y_s.at[0])
    wait(bo, s_y_r.at[0])
    for ch, (c0, cw) in enumerate(CHUNKS):
        wait(fo.at[:, :, pl.ds(0, 4 * cw)], s_y_s.at[1 + ch])
        wait(fo.at[:, :, pl.ds(0, 4 * cw)], s_y_r.at[1 + ch])


def hand_over(fo, bo, f_out, b_out, held, sem):
    parts = [(i, pl.ds(4 * k, 4)) for i in (0, 1) for k in (0, 1)]
    loads = [pltpu.make_async_copy((fo, bo)[i].at[at], held.at[i, at], sem.at[0, n]) for n, (i, at) in enumerate(parts)]
    stores = [pltpu.make_async_copy(held.at[i, at], (f_out, b_out)[i].at[at], sem.at[1, n]) for n, (i, at) in enumerate(parts)]
    for copy in loads:
        copy.start()
    for load, store in zip(loads, stores):
        load.wait()
        store.start()
    for copy in stores:
        copy.wait()


def local(
    forward_input,
    forward_routes,
    forward_gates,
    backward_input,
    backward_routes,
    backward_gates,
    upstream_gradient,
    norm_gain,
    gate_weight,
    up_weight,
    down_weight,
):
    shape = (8, 16, D)
    parts = 1 + len(CHUNKS)
    groups = 2 * len(CHUNKS)
    dma = pltpu.SemaphoreType.DMA
    anywhere = pl.BlockSpec(memory_space=pl.ANY)
    fo, bo = pl.pallas_call(
        kernel,
        name="relay",
        out_shape=(jax.ShapeDtypeStruct(shape, BF), jax.ShapeDtypeStruct(shape, BF)),
        in_specs=[anywhere] * 11,
        out_specs=(anywhere, anywhere),
        scratch_shapes=[
            pltpu.VMEM((D, FE), BF),
            pltpu.VMEM((D, FE), BF),
            pltpu.VMEM((FE, D), BF),
            pltpu.VMEM((3, 2, 8, 8, 16, QUARTER), BF),
            pltpu.VMEM((3, 28, 16, HALF), BF),
            pltpu.VMEM((3, 28, 16, HALF), BF),
            pltpu.VMEM((2, 2, 8, 8, 16, QUARTER), BF),
            pltpu.VMEM((2, 8, 8, 16, QUARTER), BF),
            pltpu.VMEM((3, 8, 16, D), BF),
            pltpu.VMEM((2, 8, 8, 128), F32),
            pltpu.VMEM((2, 2, 8, 128, 128), BF),
            pltpu.VMEM((2, 2, 8, 128, 128), BF),
            pltpu.VMEM((448, FE), BF),
            pltpu.VMEM((448, FE), BF),
            pltpu.VMEM((448, FE), F32),
            pltpu.VMEM((448, 448), BF),
            pltpu.VMEM((2, 8, 128, 256), BF),
            pltpu.VMEM((2, 2, 8, 128, 256), BF),
            pltpu.VMEM((8, 128), F32),
            pltpu.VMEM((2, 128), jnp.int32),
            pltpu.VMEM((2, 128), F32),
            pltpu.VMEM((2, 128), jnp.int32),
            pltpu.VMEM((2, 128), F32),
            pltpu.VMEM((1, D), BF),
            dma((2,)),
            dma((2,)),
            dma((3, 2, 6)),
            dma((3, 2)),
            dma((3, 2)),
            dma((3, 2)),
            dma((groups, 2)),
            dma((groups, 2)),
            dma((groups, 2, 2)),
            dma((groups, 2)),
            dma((groups, 2)),
            dma((groups, 2)),
            dma((groups, 2, 2)),
            dma((parts,)),
            dma((parts,)),
            dma((3,)),
            dma((3,)),
            dma((3, 2)),
            dma((5,)),
        ],
        compiler_params=pltpu.CompilerParams(
            collective_id=0, has_side_effects=True, vmem_limit_bytes=64 * 1024 * 1024 - 65536
        ),
        cost_estimate=pl.CostEstimate(flops=46 * 10**9, bytes_accessed=30 * 10**6, transcendentals=10**6),
    )(
        forward_routes[0].T,
        forward_gates[0].T,
        backward_routes[0].T,
        backward_gates[0].T,
        forward_input.reshape(shape),
        backward_input.reshape(shape),
        upstream_gradient.reshape(shape),
        norm_gain,
        gate_weight[0, 0],
        up_weight[0, 0],
        down_weight[0, 0],
    )
    fo, bo = pl.pallas_call(
        hand_over,
        name="results",
        out_shape=(jax.ShapeDtypeStruct(shape, BF), jax.ShapeDtypeStruct(shape, BF)),
        in_specs=[anywhere] * 2,
        out_specs=(anywhere, anywhere),
        scratch_shapes=[pltpu.VMEM((2,) + shape, BF), dma((2, 4))],
        cost_estimate=pl.CostEstimate(flops=0, bytes_accessed=4 * 10**6, transcendentals=0),
    )(fo, bo)
    return (fo.reshape(1, 128, D), bo.reshape(1, 128, D))


def solution(mesh):
    rows_spec = P("pipe", "expert", None)
    weight = P("pipe", "expert", None, None)
    in_specs = (rows_spec,) * 7 + (P("pipe", None), weight, weight, weight)
    out_specs = (rows_spec, rows_spec)
    return jax.shard_map(local, mesh=mesh, in_specs=in_specs, out_specs=out_specs, check_vma=False)
```

```python
import functools

import jax
import jax.numpy as jnp
from jax import lax
from jax.experimental import pallas as pl
from jax.experimental.pallas import tpu as pltpu
from jax.sharding import PartitionSpec as P

EPSILON = 1e-06
MESH = pl.DeviceIdType.MESH
BF = jnp.bfloat16
F32 = jnp.float32
D = 3584
FE = 1024
HALF = D // 2
QUARTER = D // 4
SIDE = 4
SLOTS = 14
CHUNKS = ((0, 384), (384, 256), (640, 128), (768, 128))
DIRECT = (2, 3)
PARTS = ((0, 3), (3, 1))
STEP = 256
WIDE = 512


def dot(a, b):
    return jnp.dot(a, b, preferred_element_type=F32)


def dot_nt(a, b):
    return lax.dot_general(a, b, (((1,), (1,)), ((), ())), preferred_element_type=F32)


def rows(value):
    return value.reshape(value.shape[-3] * value.shape[-2], value.shape[-1])


def tiles(value):
    return value.reshape(value.shape[0] // 16, 16, value.shape[1])


def split(value):
    high = value.astype(BF)
    return high, (value - high.astype(F32)).astype(BF)


def kernel(
    fr_in, fg_in, br_in, bg_in, fin, bin_, upg, gain_in, wg, wu, wd, fo, bo,
    WG, WU, WD, G, XA, YB, S, L, OWN, RG, PA, PB, GG, UG, HID, PERM, PT, PG, rg, fr, fg, br, bg, gain,
    s_rg_r, s_rg_s, s_g_r, s_g_s, s_x_r, s_x_s, s_r_r, s_r_s,
    s_t1_r, s_t1_s, s_t2_r, s_t2_s, s_c_r, s_y_r, s_y_s, s_w, s_o, s_l, s_i,
):
    pipe = lax.axis_index("pipe")
    me = lax.axis_index("expert")
    core = lax.rem(me, 2)
    other = 1 - core
    ring = (lax.rem(me // 2, SIDE), me // (2 * SIDE))
    X = (XA, YB)

    def at(h, delta):
        return lax.rem(ring[h] + delta, SIDE)

    def dev(h, delta, k):
        r = at(h, delta)
        if h == 0:
            return (pipe, (ring[1] * SIDE + r) * 2 + k)
        return (pipe, (r * SIDE + ring[0]) * 2 + k)

    def cols(h, q, c0=0, cw=QUARTER):
        return pl.ds(pl.multiple_of(h * HALF + q * QUARTER + c0, 128), cw)

    def qcols(q, c0=0, cw=QUARTER):
        return pl.ds(pl.multiple_of(q * QUARTER + c0, 128), cw)

    def send(src, dst, ss, rs, device):
        pltpu.make_async_remote_copy(
            src_ref=src, dst_ref=dst, send_sem=ss, recv_sem=rs, device_id=device, device_id_type=MESH
        ).start()

    def copy(src, dst, sem):
        pltpu.make_async_copy(src, dst, sem).start()

    def wait(ref, sem):
        pltpu.make_async_copy(ref, ref, sem).wait()

    barrier = pltpu.get_barrier_semaphore()
    peers = [dev(h, d, k) for h in (0, 1) for d in (1, 2, 3) for k in (0, 1)]
    peers.append(dev(0, 0, other))
    ahead = (lax.rem(pipe + 1, SIDE), me)
    behind = (lax.rem(pipe + 3, SIDE), me)
    peers += [ahead, behind]
    for peer in peers:
        pl.semaphore_signal(barrier, inc=1, device_id=peer, device_id_type=MESH)
    def normalize(a):
        def body(k, carry):
            v = OWN[a, k].astype(F32)
            r = lax.rsqrt(jnp.mean(v * v, axis=-1, keepdims=True) + EPSILON)
            OWN[a, k] = (v * r * gain[...].astype(F32)).astype(BF)
            return carry

        lax.fori_loop(0, 8, body, 0)

    copy(upg, OWN.at[0], s_o.at[0])
    copy(bin_, OWN.at[1], s_o.at[1])
    copy(fin, OWN.at[2], s_o.at[2])

    small = ((fr_in, fr), (fg_in, fg), (br_in, br), (bg_in, bg), (gain_in, gain))
    for n, (src, dst) in enumerate(small):
        copy(src, dst, s_i.at[n])
    for n, (src, dst) in enumerate(small):
        wait(dst, s_i.at[n])
    rg[pl.ds(0, 2), :] = fr[...].astype(F32)
    rg[pl.ds(2, 2), :] = fg[...]
    rg[pl.ds(4, 2), :] = br[...].astype(F32)
    rg[pl.ds(6, 2), :] = bg[...]

    up = lax.broadcasted_iota(jnp.int32, (128, 128), 0)
    across = lax.broadcasted_iota(jnp.int32, (128, 128), 1)
    triangle = jnp.where(up < across, 1.0, 0.0).astype(BF)
    identity = jnp.where(up == across, 1.0, 0.0).astype(BF)
    line = lax.broadcasted_iota(jnp.int32, (448, 448), 0)
    outer = (line >= 112).astype(jnp.int32) + (line >= 224).astype(jnp.int32) + (line >= 336).astype(jnp.int32)
    rest = line - 112 * outer
    inner = (rest >= 28).astype(jnp.int32) + (rest >= 56).astype(jnp.int32) + (rest >= 84).astype(jnp.int32)
    place = 112 * inner + 28 * outer + rest - 28 * inner
    PERM[...] = jnp.where(lax.broadcasted_iota(jnp.int32, (448, 448), 1) == place, 1.0, 0.0).astype(BF)

    pl.semaphore_wait(barrier, len(peers))

    for h in (0, 1):
        mine = ring[h] * 2 + core
        for d in (1, 2, 3):
            for k in (0, 1):
                send(rg, RG.at[h, mine], s_rg_s.at[h], s_rg_r.at[h], dev(h, d, k))
        send(rg, RG.at[h, mine], s_rg_s.at[h], s_rg_r.at[h], dev(h, 0, other))
        copy(rg, RG.at[h, mine], s_rg_r.at[h])

    def gather_start(a):
        for h in (0, 1):
            mine = ring[h] * 2 + core
            for d, k in ((1, 0), (3, 1)):
                for q in (0, 1):
                    send(OWN.at[a, :, :, cols(h, q)], G.at[a, h, mine], s_g_s.at[a, h], s_g_r.at[a, h, k], dev(h, d, q))
            send(OWN.at[a, :, :, cols(h, other)], G.at[a, h, mine], s_g_s.at[a, h], s_g_r.at[a, h, 4], dev(h, 0, other))
            copy(OWN.at[a, :, :, cols(h, core)], G.at[a, h, mine], s_g_r.at[a, h, 5])

    def gather_forward(a):
        for h in (0, 1):
            left = 2 * at(h, 3)
            wait(G.at[a, h, pl.ds(left, 2)], s_g_r.at[a, h, 0])
            for k in (0, 1):
                part = G.at[a, h, left + k, pl.ds(0, 4)]
                send(part, part, s_g_s.at[a, h], s_g_r.at[a, h, 2], dev(h, 1, core))
        for h in (0, 1):
            right = 2 * at(h, 1)
            wait(G.at[a, h, pl.ds(right, 2)], s_g_r.at[a, h, 1])
            for k in (0, 1):
                part = G.at[a, h, right + k, pl.ds(4, 4)]
                send(part, part, s_g_s.at[a, h], s_g_r.at[a, h, 3], dev(h, 3, core))

    def gather_finish(a, h):
        far = 2 * at(h, 2)
        wait(G.at[a, h, pl.ds(far, 2), pl.ds(0, 4)], s_g_r.at[a, h, 2])
        wait(G.at[a, h, pl.ds(far, 2), pl.ds(4, 4)], s_g_r.at[a, h, 3])
        wait(G.at[a, h, ring[h] * 2 + other], s_g_r.at[a, h, 4])
        wait(G.at[a, h, ring[h] * 2 + core], s_g_r.at[a, h, 5])

    def gather_sent(a):
        for h in (0, 1):
            wait(G.at[a, h, pl.ds(0, 7)], s_g_s.at[a, h])

    wait(OWN.at[0], s_o.at[0])
    gather_start(0)
    wait(OWN.at[1], s_o.at[1])
    normalize(1)
    copy(wd, WD, s_w.at[2])
    copy(wg, WG, s_w.at[0])
    copy(wu, WU, s_w.at[1])
    wait(OWN.at[2], s_o.at[2])
    normalize(2)

    def experts(h):
        e = up // 16
        if h == 0:
            ids = (e // 2) * (2 * SIDE) + ring[0] * 2 + e % 2
        else:
            ids = ring[1] * (2 * SIDE) + e
        return ids.astype(F32)

    ids = [experts(h) for h in (0, 1)]
    in_tile = (up % 16).astype(F32)

    def route_row(h, s, row):
        return RG[h, s, pl.ds(row, 1), :]

    def build(st, h):
        def body(s, carry):
            named = (route_row(h, s, 4 * st) == ids[h]) | (route_row(h, s, 4 * st + 1) == ids[h])
            mask = jnp.where(named, 1.0, 0.0)
            before = dot(mask.astype(BF), triangle)
            first = 2.0 * s.astype(F32) + in_tile
            PA[st, h, s] = jnp.where(before == first, mask, 0.0).astype(BF)
            PB[st, h, s] = jnp.where(before == first - 16.0, mask, 0.0).astype(BF)
            return carry

        lax.fori_loop(0, 8, body, 0)

    def gates(st, h, s):
        return jnp.where(route_row(h, s, 4 * st) == ids[h], route_row(h, s, 4 * st + 2), route_row(h, s, 4 * st + 3))

    for h in (0, 1):
        wait(RG.at[h], s_rg_r.at[h])
    for h in (0, 1):
        build(1, h)
    gather_start(1)
    for h in (0, 1):
        build(0, h)

    def pack(a, st, h, b, gated):
        def body(i, carry):
            both = rows(G[a, h, pl.ds(i, 2)].reshape(16, 16, QUARTER))
            pick = jnp.concatenate([PA[st, h, i], PB[st, h, i + 1]], axis=1)
            if gated:
                weight = jnp.concatenate([gates(st, h, i), gates(st, h, i + 1)], axis=1)
                high, low = split(pick.astype(F32) * weight)
                out = dot(high, both) + dot(low, both)
            else:
                out = dot(pick, both)
            S[b, h, :, i] = tiles(out.astype(BF))
            return carry

        lax.fori_loop(0, 7, body, 0)

    def scatter_start(a, h, b):
        place_at = pl.ds(7 * ring[1 - h], 7)
        for d in (1, 3, 2):
            for k in (0, 1):
                send(
                    S.at[b, h, 2 * at(1 - h, d) + k, pl.ds(0, 7)], X[h].at[a, place_at, :, qcols(core)],
                    s_x_s.at[a, h], s_x_r.at[a, h], dev(1 - h, d, k),
                )
        send(
            S.at[b, h, 2 * ring[1 - h] + other, pl.ds(0, 7)], X[h].at[a, place_at, :, qcols(core)],
            s_x_s.at[a, h], s_x_r.at[a, h], dev(1 - h, 0, other),
        )
        copy(S.at[b, h, 2 * ring[1 - h] + core, pl.ds(0, 7)], X[h].at[a, place_at, :, qcols(core)], s_l.at[a, h])

    def scatter_sent(a, b):
        for h in (0, 1):
            wait(S.at[b, h, pl.ds(0, 7), pl.ds(0, 7)], s_x_s.at[a, h])
            wait(S.at[b, h, 0, pl.ds(0, 7)], s_l.at[a, h])

    def scatter_finish(a, b):
        for h in (0, 1):
            wait(S.at[b, h, pl.ds(0, 7), pl.ds(0, 7)], s_x_r.at[a, h])

    gather_forward(0)
    for h in (0, 1):

        def turn(s, carry):
            for k, T in enumerate((PB, PA)):
                spot = pl.ds(128 * k, 128)
                PT[h, s, :, spot] = dot_nt(identity, T[1, h, s]).astype(BF)
                for n, part in enumerate(split(T[0, h, s].astype(F32) * gates(0, h, s))):
                    PG[n, h, s, :, spot] = dot_nt(identity, part).astype(BF)
            return carry

        lax.fori_loop(0, 8, turn, 0)

    gather_forward(1)
    gather_start(2)
    for h in (0, 1):
        gather_finish(0, h)
        pack(0, 1, h, 0, True)
        scatter_start(0, h, 0)
    gather_sent(0)
    for h in (0, 1):
        gather_finish(1, h)
        pack(1, 1, h, 1, False)
    gather_forward(2)
    for h in (0, 1):
        scatter_start(1, h, 1)
    gather_sent(1)
    scatter_sent(0, 0)
    for h in (0, 1):
        gather_finish(2, h)
        pack(2, 0, h, 0, False)
    gather_sent(2)
    for h in (0, 1):
        scatter_start(2, h, 0)

    def exchange(a):
        def body(n, carry):
            at_cols = pl.ds(pl.multiple_of(n * 896, 896), 896)
            YB[a, :, :, at_cols] = tiles(dot(PERM[...], rows(YB[a, :, :, at_cols])).astype(BF))
            return carry

        lax.fori_loop(0, HALF // 896, body, 0)

    def exchange_hidden(src, dst):
        def body(n, carry):
            at_cols = pl.ds(pl.multiple_of(n * WIDE, WIDE), WIDE)
            dst[1, :, :, at_cols] = tiles(dot(PERM[...], src[:, at_cols]).astype(BF))
            return carry

        lax.fori_loop(0, FE // WIDE, body, 0)

    scatter_finish(0, 0)
    exchange(0)
    wait(WD, s_w.at[2])

    def early_hidden(f, carry):
        at_cols = pl.ds(pl.multiple_of(f * STEP, STEP), STEP)
        HID[:, at_cols] = dot_nt(rows(XA[0]), WD[at_cols, pl.ds(0, HALF)]) + dot_nt(rows(YB[0]), WD[at_cols, pl.ds(HALF, HALF)])
        return carry

    lax.fori_loop(0, FE // STEP, early_hidden, 0)
    wait(WG, s_w.at[0])
    wait(WU, s_w.at[1])
    scatter_finish(1, 1)
    scatter_sent(1, 1)
    exchange(1)

    def into(a, W, at_cols):
        return dot(rows(XA[a]), W[pl.ds(0, HALF), at_cols]) + dot(rows(YB[a]), W[pl.ds(HALF, HALF), at_cols])

    def backward_hidden(f, carry):
        at_cols = pl.ds(pl.multiple_of(f * STEP, STEP), STEP)
        pre_gate = into(1, WG, at_cols)
        pre_up = into(1, WU, at_cols)
        hidden = HID[:, at_cols]
        sig = 1.0 / (1.0 + jnp.exp(-pre_gate))
        GG[:, at_cols] = (hidden * pre_up * sig * (1.0 + pre_gate * (1.0 - sig))).astype(BF)
        UG[:, at_cols] = (hidden * pre_gate * sig).astype(BF)
        return carry

    lax.fori_loop(0, FE // STEP, backward_hidden, 0)
    exchange_hidden(GG, XA)
    exchange_hidden(UG, YB)

    def return_start(b, ch, h, a, quarters=(0, 1), home=True):
        c0, cw = (0, QUARTER) if b == 0 else CHUNKS[ch]
        mine = 2 * ring[1 - h] + core
        n = b * len(CHUNKS) + ch
        dst = G.at[b, h, pl.ds(0, 7), mine, :, pl.ds(c0, cw)]
        for d in (1, 3, 2):
            for q in quarters:
                send(
                    X[h].at[a, pl.ds(7 * at(1 - h, d), 7), :, qcols(q, c0, cw)], dst,
                    s_r_s.at[n, h], s_r_r.at[n, h], dev(1 - h, d, q),
                )
        if home:
            here = pl.ds(7 * ring[1 - h], 7)
            send(X[h].at[a, here, :, qcols(other, c0, cw)], dst, s_r_s.at[n, h], s_r_r.at[n, h], dev(1 - h, 0, other))
            copy(X[h].at[a, here, :, qcols(core, c0, cw)], dst, s_r_r.at[n, h])

    def backward_out(h, first, last):
        def body(n, carry):
            at_rows = pl.ds(pl.multiple_of(h * HALF + n * STEP, STEP), STEP)
            at_cols = pl.ds(pl.multiple_of(n * STEP, STEP), STEP)
            if h == 0:
                gg, ug = GG[...], UG[...]
            else:
                gg, ug = rows(XA[1, :, :, pl.ds(0, FE)]), rows(YB[1, :, :, pl.ds(0, FE)])
            X[h][0, :, :, at_cols] = tiles((dot_nt(gg, WG[at_rows, :]) + dot_nt(ug, WU[at_rows, :])).astype(BF))
            return carry

        lax.fori_loop(first, last, body, 0)

    for q, first, last in ((0, 0, 4), (1, 4, HALF // STEP)):
        for h in (0, 1):
            backward_out(h, first, last)
        for h in (0, 1):
            return_start(0, 0, h, 0, (q,), q == 1)

    scatter_finish(2, 0)
    scatter_sent(2, 0)
    exchange(2)

    def forward_hidden(f, carry):
        at_cols = pl.ds(pl.multiple_of(f * STEP, STEP), STEP)
        pre_gate = into(2, WG, at_cols)
        pre_up = into(2, WU, at_cols)
        GG[:, at_cols] = (pre_gate * pre_up / (1.0 + jnp.exp(-pre_gate))).astype(BF)
        return carry

    lax.fori_loop(0, FE // STEP, forward_hidden, 0)
    exchange_hidden(GG, XA)
    def forward_out(ch):
        c0, cw = CHUNKS[ch]
        for h in (0, 1):
            for q in (0, 1):
                for n in range(0, cw, STEP):
                    w = min(STEP, cw - n)
                    act = GG[...] if h == 0 else rows(XA[1, :, :, pl.ds(0, FE)])
                    start = q * QUARTER + c0 + n
                    X[h][2, :, :, pl.ds(start, w)] = tiles(dot(act, WD[:, pl.ds(h * HALF + start, w)]).astype(BF))

    def forward_return(ch):
        for h in (0, 1):
            return_start(1, ch, h, 2)

    forward_out(0)
    forward_return(0)

    copy(bin_, OWN.at[1], s_o.at[1])
    copy(fin, OWN.at[2], s_o.at[2])

    def combine(b, ch, h, ds):
        c0, cw = (0, QUARTER) if b == 0 else CHUNKS[ch]
        to = 1 if b == 0 else 0
        here = pl.ds(c0, cw)
        for d in ds:
            for k in (0, 1):
                s = 2 * at(h, d) + k
                prev = rows(G[b, h, jnp.maximum(s - 1, 0), :, :, here])
                cur = rows(G[b, h, jnp.minimum(s, 6), :, :, here])
                both = jnp.concatenate([prev, cur], axis=0)
                if b == 0:
                    out = dot(PT[h, s], both)
                else:
                    out = dot(PG[0, h, s], both) + dot(PG[1, h, s], both)
                S[to, h, s, :, :, here] = tiles(out.astype(BF))

    def land(b):
        return L if b == 0 else G.at[2]

    def meta(b, ch):
        c0, cw = (0, QUARTER) if b == 0 else CHUNKS[ch]
        return b * len(CHUNKS) + ch, pl.ds(c0, cw), (1 if b == 0 else 0), land(b)

    def far_start(b, ch, h):
        n, here, to, B = meta(b, ch)
        far = 2 * at(h, 2)
        combine(b, ch, h, (2,))
        for k in (0, 1):
            send(S.at[to, h, far + k, pl.ds(0, 4), :, here], B.at[h, 6, pl.ds(4 * k, 4), :, here], s_t1_s.at[n, h], s_t1_r.at[n, h, 0], dev(h, 1, core))
            send(S.at[to, h, far + k, pl.ds(4, 4), :, here], B.at[h, 7, pl.ds(4 * k, 4), :, here], s_t1_s.at[n, h], s_t1_r.at[n, h, 1], dev(h, 3, core))

    def own_start(b, ch, h, ds=(1, 3, 0)):
        n, here, to, B = meta(b, ch)
        combine(b, ch, h, ds)
        send(S.at[to, h, 2 * ring[h] + other, :, :, here], B.at[h, 4 + core, :, :, here], s_t2_s.at[n, h], s_c_r.at[n, h, 0], dev(h, 0, other))
        copy(S.at[to, h, 2 * ring[h] + core, :, :, here], B.at[h, 4 + core, :, :, here], s_c_r.at[n, h, 1])

    def near_start(b, ch, h):
        n, here, to, B = meta(b, ch)
        for slot, d, t0, base in ((6, 1, 0, 0), (7, 3, 4, 2)):
            wait(B.at[h, slot, :, :, here], s_t1_r.at[n, h, slot - 6])
            near = 2 * at(h, d)
            for k in (0, 1):
                own = S[to, h, near + k, pl.ds(t0, 4), :, here].astype(F32)
                got = B[h, slot, pl.ds(4 * k, 4), :, here].astype(F32)
                S[to, h, near + k, pl.ds(t0, 4), :, here] = (own + got).astype(BF)
                send(S.at[to, h, near + k, :, :, here], B.at[h, base + core, :, :, here], s_t2_s.at[n, h], s_t2_r.at[n, h], dev(h, d, k))

    def stored_near(part):
        n, here, to, B = meta(0, 0)
        start, size = PARTS[part]
        for h in (0, 1):
            for slot, d, t0, base in ((6, 1, 0, 0), (7, 3, 4, 2)):
                if part == 0:
                    wait(B.at[h, slot], s_t1_r.at[n, h, slot - 6])
                near = 2 * at(h, d)
                for k in (0, 1):
                    first = pl.ds(t0 + start, size)
                    own = S[to, h, near + k, first].astype(F32)
                    got = B[h, slot, pl.ds(4 * k + start, size)].astype(F32)
                    S[to, h, near + k, first] = (own + got).astype(BF)
                    for t in (0, 4):
                        both = pl.ds(t + start, size)
                        send(S.at[to, h, near + k, both], B.at[h, base + core, both], s_t2_s.at[part, h], s_t2_r.at[part, h], dev(h, d, k))

    def stored_finish(part):
        n, here, to, B = meta(0, 0)
        for h in (0, 1):
            wait(B.at[h, pl.ds(0, PARTS[part][1])], s_t2_r.at[part, h])
            if part == 0:
                wait(B.at[h, 4 + other], s_c_r.at[n, h, 0])
                wait(B.at[h, 4 + core], s_c_r.at[n, h, 1])

    def pieces(ch):
        return 2 if ch == len(CHUNKS) - 1 else 1

    def piece(ch, part):
        size = 8 // pieces(ch)
        return (2 if part == 1 else len(CHUNKS) + ch), pl.ds(size * part, size)

    def relay_direct(ch):
        n, here, to, B = meta(1, ch)
        for h in (0, 1):
            wait(G.at[1, h, pl.ds(0, 7), :, :, here], s_r_r.at[n, h])
        for part in range(pieces(ch)):
            m, some = piece(ch, part)
            for d, base in ((2, 6), (1, 0), (3, 2)):
                for h in (0, 1):
                    if part == 0:
                        combine(1, ch, h, (d,))
                    for k in (0, 1):
                        ss, rs = (s_t1_s.at[m, h], s_t1_r.at[m, h, 0]) if d == 2 else (s_t2_s.at[m, h], s_t2_r.at[m, h])
                        send(S.at[to, h, 2 * at(h, d) + k, some, :, here], B.at[h, base + core, some, :, here], ss, rs, dev(h, d, k))
        for h in (0, 1):
            own_start(1, ch, h, (0,))

    def near_finish(ch, h, part):
        n, here, to, B = meta(1, ch)
        m, some = piece(ch, part)
        if ch in DIRECT:
            wait(B.at[h, pl.ds(6, 2), some, :, here], s_t1_r.at[m, h, 0])
        wait(B.at[h, pl.ds(0, 4), some, :, here], s_t2_r.at[m, h])
        if part == 0:
            wait(B.at[h, 4 + other, :, :, here], s_c_r.at[n, h, 0])
            wait(B.at[h, 4 + core, :, :, here], s_c_r.at[n, h, 1])

    def arrived(b, h, q, k, here, direct=False):
        B = land(b)
        far = B[h, 6 + q, k, :, here].astype(F32) if direct else 0.0
        return far + B[h, q, k, :, here].astype(F32) + B[h, 2 + q, k, :, here].astype(F32) + B[h, 4 + q, k, :, here].astype(F32)

    for h in (0, 1):
        wait(G.at[0, h, pl.ds(0, 7)], s_r_r.at[0, h])
        far_start(0, 0, h)
    for h in (0, 1):
        own_start(0, 0, h)
    def relay_far(ch):
        n, here, to, B = meta(1, ch)
        for h in (0, 1):
            wait(G.at[1, h, pl.ds(0, 7), :, :, here], s_r_r.at[n, h])
            far_start(1, ch, h)
        for h in (0, 1):
            own_start(1, ch, h)

    def relay_near(ch):
        for h in (0, 1):
            near_start(1, ch, h)

    forward_out(1)
    relay_far(0)
    forward_return(1)
    forward_out(2)
    forward_out(3)
    stored_near(0)
    relay_near(0)
    relay_far(1)
    forward_return(2)

    def forward_last(ch):
        c0, cw = CHUNKS[ch]
        n, here, to, B = meta(1, ch)
        size = 8 // pieces(ch)
        for part in range(pieces(ch)):
            some = pl.ds(size * part, size)
            for h in (0, 1):
                near_finish(ch, h, part)

                def body(k, carry):
                    for q in (0, 1):
                        spot = pl.ds(h * HALF + q * QUARTER + c0, cw)
                        OWN[2, k, :, spot] = (OWN[2, k, :, spot].astype(F32) + arrived(1, h, q, k, here, ch in DIRECT)).astype(BF)
                    return carry

                lax.fori_loop(size * part, size * part + size, body, 0)
                for q in (0, 1):
                    spot = pl.ds(h * HALF + q * QUARTER + c0, cw)
                    send(OWN.at[2, some, :, spot], fo.at[some, :, spot], s_y_s.at[1 + ch], s_y_r.at[1 + ch], ahead)

    def backward_last(k, carry):
        summed = jnp.concatenate([arrived(0, h, q, k, pl.ds(0, QUARTER)) for h in (0, 1) for q in (0, 1)], axis=1)
        stored = OWN[1, k].astype(F32)
        r = lax.rsqrt(jnp.mean(stored * stored, axis=-1, keepdims=True) + EPSILON)
        grad = gain[...].astype(F32) * summed
        mean = jnp.mean(stored * grad, axis=-1, keepdims=True)
        OWN[1, k] = (OWN[0, k].astype(F32) + r * grad - stored * (r * r * r) * mean).astype(BF)
        return carry

    def stored_last(part):
        stored_finish(part)
        start, size = PARTS[part]
        for first in (start, 4 + start):
            lax.fori_loop(first, first + size, backward_last, 0)
            both = pl.ds(first, size)
            send(OWN.at[1, both], bo.at[both], s_y_s.at[0], s_y_r.at[0], behind)

    wait(OWN.at[1], s_o.at[1])
    wait(OWN.at[2], s_o.at[2])
    stored_last(0)
    forward_last(0)
    relay_near(1)
    forward_return(3)
    stored_near(1)
    relay_direct(2)
    forward_last(1)
    relay_direct(3)
    stored_last(1)
    forward_last(2)
    forward_last(3)

    for h in (0, 1):
        wait(RG.at[h, pl.ds(0, 7)], s_rg_s.at[h])
    for b, chunks in ((0, ((0, QUARTER),)), (1, CHUNKS)):
        for ch, (c0, cw) in enumerate(chunks):
            n, here, to, B = meta(b, ch)
            for h in (0, 1):
                wait(S.at[to, h, pl.ds(0, 7), pl.ds(0, 7), :, here], s_r_s.at[n, h])
                if b == 0:
                    wait(S.at[to, h, pl.ds(0, 2)], s_t1_s.at[n, h])
                    wait(S.at[to, h, pl.ds(0, 1 + PARTS[0][1])], s_t2_s.at[n, h])
                    wait(S.at[to, h, pl.ds(0, PARTS[1][1])], s_t2_s.at[1, h])
                elif pieces(ch) == 1:
                    wait(S.at[to, h, pl.ds(0, 2), :, :, here], s_t1_s.at[n, h])
                    wait(S.at[to, h, pl.ds(0, 5), :, :, here], s_t2_s.at[n, h])
                else:
                    wait(S.at[to, h, pl.ds(0, 1), :, :, here], s_t1_s.at[n, h])
                    wait(S.at[to, h, pl.ds(0, 3), :, :, here], s_t2_s.at[n, h])
                    wait(S.at[to, h, pl.ds(0, 1), :, :, here], s_t1_s.at[2, h])
                    wait(S.at[to, h, pl.ds(0, 2), :, :, here], s_t2_s.at[2, h])
    wait(bo, s_y_s.at[0])
    wait(bo, s_y_r.at[0])
    for ch, (c0, cw) in enumerate(CHUNKS):
        wait(fo.at[:, :, pl.ds(0, 4 * cw)], s_y_s.at[1 + ch])
        wait(fo.at[:, :, pl.ds(0, 4 * cw)], s_y_r.at[1 + ch])


def hand_over(fo, bo, f_out, b_out, held, sem):
    parts = [(i, pl.ds(4 * k, 4)) for i in (0, 1) for k in (0, 1)]
    loads = [pltpu.make_async_copy((fo, bo)[i].at[at], held.at[i, at], sem.at[0, n]) for n, (i, at) in enumerate(parts)]
    stores = [pltpu.make_async_copy(held.at[i, at], (f_out, b_out)[i].at[at], sem.at[1, n]) for n, (i, at) in enumerate(parts)]
    for copy in loads:
        copy.start()
    for load, store in zip(loads, stores):
        load.wait()
        store.start()
    for copy in stores:
        copy.wait()


def local(
    forward_input,
    forward_routes,
    forward_gates,
    backward_input,
    backward_routes,
    backward_gates,
    upstream_gradient,
    norm_gain,
    gate_weight,
    up_weight,
    down_weight,
):
    shape = (8, 16, D)
    parts = 1 + len(CHUNKS)
    groups = 2 * len(CHUNKS)
    dma = pltpu.SemaphoreType.DMA
    anywhere = pl.BlockSpec(memory_space=pl.ANY)
    fo, bo = pl.pallas_call(
        kernel,
        name="relay",
        out_shape=(jax.ShapeDtypeStruct(shape, BF), jax.ShapeDtypeStruct(shape, BF)),
        in_specs=[anywhere] * 11,
        out_specs=(anywhere, anywhere),
        scratch_shapes=[
            pltpu.VMEM((D, FE), BF),
            pltpu.VMEM((D, FE), BF),
            pltpu.VMEM((FE, D), BF),
            pltpu.VMEM((3, 2, 8, 8, 16, QUARTER), BF),
            pltpu.VMEM((3, 28, 16, HALF), BF),
            pltpu.VMEM((3, 28, 16, HALF), BF),
            pltpu.VMEM((2, 2, 8, 8, 16, QUARTER), BF),
            pltpu.VMEM((2, 8, 8, 16, QUARTER), BF),
            pltpu.VMEM((3, 8, 16, D), BF),
            pltpu.VMEM((2, 8, 8, 128), F32),
            pltpu.VMEM((2, 2, 8, 128, 128), BF),
            pltpu.VMEM((2, 2, 8, 128, 128), BF),
            pltpu.VMEM((448, FE), BF),
            pltpu.VMEM((448, FE), BF),
            pltpu.VMEM((448, FE), F32),
            pltpu.VMEM((448, 448), BF),
            pltpu.VMEM((2, 8, 128, 256), BF),
            pltpu.VMEM((2, 2, 8, 128, 256), BF),
            pltpu.VMEM((8, 128), F32),
            pltpu.VMEM((2, 128), jnp.int32),
            pltpu.VMEM((2, 128), F32),
            pltpu.VMEM((2, 128), jnp.int32),
            pltpu.VMEM((2, 128), F32),
            pltpu.VMEM((1, D), BF),
            dma((2,)),
            dma((2,)),
            dma((3, 2, 6)),
            dma((3, 2)),
            dma((3, 2)),
            dma((3, 2)),
            dma((groups, 2)),
            dma((groups, 2)),
            dma((groups, 2, 2)),
            dma((groups, 2)),
            dma((groups, 2)),
            dma((groups, 2)),
            dma((groups, 2, 2)),
            dma((parts,)),
            dma((parts,)),
            dma((3,)),
            dma((3,)),
            dma((3, 2)),
            dma((5,)),
        ],
        compiler_params=pltpu.CompilerParams(
            collective_id=0, has_side_effects=True, vmem_limit_bytes=64 * 1024 * 1024 - 65536
        ),
        cost_estimate=pl.CostEstimate(flops=46 * 10**9, bytes_accessed=30 * 10**6, transcendentals=10**6),
    )(
        forward_routes[0].T,
        forward_gates[0].T,
        backward_routes[0].T,
        backward_gates[0].T,
        forward_input.reshape(shape),
        backward_input.reshape(shape),
        upstream_gradient.reshape(shape),
        norm_gain,
        gate_weight[0, 0],
        up_weight[0, 0],
        down_weight[0, 0],
    )
    fo, bo = pl.pallas_call(
        hand_over,
        name="results",
        out_shape=(jax.ShapeDtypeStruct(shape, BF), jax.ShapeDtypeStruct(shape, BF)),
        in_specs=[anywhere] * 2,
        out_specs=(anywhere, anywhere),
        scratch_shapes=[pltpu.VMEM((2,) + shape, BF), dma((2, 4))],
        cost_estimate=pl.CostEstimate(flops=0, bytes_accessed=4 * 10**6, transcendentals=0),
    )(fo, bo)
    return (fo.reshape(1, 128, D), bo.reshape(1, 128, D))


def solution(mesh):
    rows_spec = P("pipe", "expert", None)
    weight = P("pipe", "expert", None, None)
    in_specs = (rows_spec,) * 7 + (P("pipe", None), weight, weight, weight)
    out_specs = (rows_spec, rows_spec)
    return jax.shard_map(local, mesh=mesh, in_specs=in_specs, out_specs=out_specs, check_vma=False)
```
